32 devices in a mesh: seg: 8 (over z, x), sample: 4 (over y, core).
Axes of the slice: x: 2, y: 2, z: 4, core: 2. Of those that a mesh axis runs over, the one named last changes fastest.
Arguments:
- queries: bfloat16 [4, 4096, 512], P('sample', 'seg'), may hold values from -6 to 6
- key_rows: bfloat16 [4, 4096, 512], P('sample', 'seg'), may hold values from -6 to 6
- value_rows: bfloat16 [4, 4096, 512], P('sample', 'seg'), may hold values from -6 to 6
- w_out: bfloat16 [512, 512], replicated, may hold values from -0.25 to 0.25
- grad_out: bfloat16 [4, 4096, 512], P('sample', 'seg'), may hold values from -6 to 6
- neighbours: int32 [4, 8, 3], P('sample', 'seg'), may hold values from 0 to 7, as said below
Outputs:
- attended: bfloat16 [4, 4096, 512], P('sample', 'seg')
- grad_queries: bfloat16 [4, 4096, 512], P('sample', 'seg')
- grad_keys: bfloat16 [4, 4096, 512], P('sample', 'seg')
- grad_values: bfloat16 [4, 4096, 512], P('sample', 'seg')
- grad_w_out: float32 [512, 512], replicated
The draws below stay inside these ranges and needn't reach their ends.
Inputs may be any that keep to these rules, and one draw needn't show every extreme that they name: `neighbours`: entries are patch indices of the same sample within 3 of the patch along the curve. Entries that differ from the patch itself are distinct and come first; entries equal to the patch itself are unused and fill the rest of the list. A patch may have 1 to 3 used entries; in every sample some patch uses all 3.
All inputs are finite; a program needn't handle non-finite values.
Results may differ from the reference program's by a relative error of at most 0.02.
Values may be sent and summed in bfloat16 or wider, within the bound.
No kernel may reach another device: no remote copies, remote signals or barrier semaphores. Data moves between devices by JAX's collectives and lax.ppermute only.
A program may use at most 128 MiB of HBM per device.

```python
import math
import jax
import jax.numpy as jnp
from jax import lax

D = 512
HEADS = 8
PATCH = 512
NBR = 3
REACH = 3
SAMPLES = 4
PATCHES = 8
TOKENS = 4096


def draw_queries(key, part):
    key = jax.random.fold_in(key, 11)
    values = jnp.clip(jax.random.normal(key, (SAMPLES, TOKENS, D), jnp.float32), -6.0, 6.0)
    return values.astype(jnp.bfloat16)


def draw_key_rows(key, part):
    key = jax.random.fold_in(key, 23)
    values = jnp.clip(jax.random.normal(key, (SAMPLES, TOKENS, D), jnp.float32), -6.0, 6.0)
    return values.astype(jnp.bfloat16)


def draw_neighbours(key, part):
    key = jax.random.fold_in(key, 37)
    key_order, key_count, key_full = jax.random.split(key, 3)
    offsets = jnp.concatenate([jnp.arange(-REACH, 0, dtype=jnp.int32), jnp.arange(1, REACH + 1, dtype=jnp.int32)])
    patch_ids = jnp.arange(PATCHES, dtype=jnp.int32)[None, :, None]
    target = patch_ids + offsets[None, None, :]
    valid = (target >= 0) & (target < PATCHES)
    ranking = jax.random.randint(key_order, (SAMPLES, PATCHES, 2 * REACH), 0, 4096) * (2 * REACH) + jnp.arange(2 * REACH, dtype=jnp.int32)
    ranking = jnp.where(valid, ranking, ranking + 2 ** 24)
    order = jnp.argsort(ranking, axis=-1)[..., :NBR]
    chosen = jnp.take_along_axis(target, order, axis=-1)
    counts = jax.random.randint(key_count, (SAMPLES, PATCHES, 1), 1, NBR + 1)
    full_patch = jax.random.randint(key_full, (SAMPLES, 1, 1), 0, PATCHES)
    counts = jnp.where(patch_ids == full_patch, NBR, counts)
    slot = jnp.arange(NBR, dtype=jnp.int32)[None, None, :]
    return jnp.where(slot < counts, chosen, patch_ids).astype(jnp.int32)


def level_of(stream_key, dims, shards, least, largest):
    gain, own = 1.0, jax.random.fold_in(stream_key, 6)
    for dim, blocks in shards:
        draws = jnp.exp(jax.random.uniform(jax.random.fold_in(own, dim), (blocks,), jnp.float32, least / len(shards), largest / len(shards)))
        gain = gain * jnp.repeat(draws, dims[dim] // blocks).reshape([-1 if axis == dim else 1 for axis in range(len(dims))])
    return gain


def gaussian(own_key, extent, scale, most, pieces=(), held_as=jnp.bfloat16):
    loudness = level_of(own_key, extent, pieces, -0.22, 0.18) if pieces else 1.0
    drawn = jax.random.normal(own_key, extent, jnp.float32) * scale * loudness
    return jnp.minimum(jnp.maximum(drawn, -most), most).astype(held_as)


def setup_inputs(seed: int = 0) -> dict:
    streams_of = jax.random.split(jax.random.key(seed), 7)
    return {
        "queries": draw_queries(jax.random.fold_in(streams_of[6], 71), 0),
        "key_rows": draw_key_rows(jax.random.fold_in(streams_of[6], 71), 0),
        "value_rows": gaussian(streams_of[2], (SAMPLES, TOKENS, D), 1.0, 6.0, ((0, 4), (1, 8))),
        "w_out": gaussian(streams_of[3], (D, D), D ** -0.5, 0.25),
        "grad_out": gaussian(streams_of[4], (SAMPLES, TOKENS, D), 1.0, 6.0, ((0, 4), (1, 8))),
        "neighbours": draw_neighbours(jax.random.fold_in(streams_of[6], 71), 0),
    }


def heads_of(matrix):
    return matrix.reshape(matrix.shape[0], HEADS, -1).transpose(1, 0, 2)

def rows_of(per_head):
    return per_head.transpose(1, 0, 2).reshape(per_head.shape[1], -1)

def rounded(values):
    return lax.optimization_barrier(values.astype(jnp.bfloat16)).astype(jnp.float32)

def attend(q_rows, key_block, value_block, key_mask, score_scale):

    def per_head(operands):
        q_head, k_head, v_head = operands
        scores = jnp.dot(q_head, k_head.T, preferred_element_type=jnp.float32) * score_scale
        scores = jnp.where(key_mask[None, :], scores, -jnp.inf)
        row_top = lax.optimization_barrier(jnp.max(scores, axis=1, keepdims=True))
        log_total = row_top + jnp.log(lax.optimization_barrier(jnp.sum(jnp.exp(scores - row_top), axis=1, keepdims=True)))
        softmax_h = jnp.exp(scores - log_total).astype(jnp.bfloat16)
        return (jnp.dot(softmax_h, v_head, preferred_element_type=jnp.float32), log_total[:, 0])
    mixture, log_total = lax.map(per_head, (heads_of(q_rows), heads_of(key_block), heads_of(value_block)))
    return (rows_of(mixture).astype(jnp.bfloat16), log_total)

def backprop(q_rows, key_block, value_block, d_attn, attn_rows, log_total, key_mask, score_scale, keep):
    row_delta = lax.optimization_barrier(jnp.sum(heads_of(d_attn).astype(jnp.float32) * heads_of(attn_rows).astype(jnp.float32), axis=-1))

    def per_head(operands):
        q_head, k_head, v_head, da_head, total_head, delta_head = operands
        scores = jnp.dot(q_head, k_head.T, preferred_element_type=jnp.float32) * score_scale
        scores = jnp.where(key_mask[None, :], scores, -jnp.inf)
        softmax_w = jnp.exp(scores - total_head[:, None])
        softmax_h = softmax_w.astype(jnp.bfloat16)
        d_prob = jnp.dot(da_head, v_head.T, preferred_element_type=jnp.float32)
        d_score = (softmax_w * (d_prob - delta_head[:, None]) * score_scale).astype(jnp.bfloat16)
        grad_q = jnp.dot(d_score, k_head, preferred_element_type=jnp.float32)
        grad_k = jnp.dot(d_score[:, :keep].T, q_head, preferred_element_type=jnp.float32)
        grad_v = jnp.dot(softmax_h[:, :keep].T, da_head, preferred_element_type=jnp.float32)
        return (grad_q, grad_k, grad_v)
    grad_q, grad_k, grad_v = lax.map(per_head, (heads_of(q_rows), heads_of(key_block), heads_of(value_block), heads_of(d_attn), log_total, row_delta))
    return (rows_of(grad_q).astype(jnp.bfloat16), rows_of(grad_k), rows_of(grad_v), row_delta)

def reference(queries, key_rows, value_rows, w_out, grad_out, neighbours):
    score_scale = 1.0 / math.sqrt(D // HEADS)

    def one_sample(operands):
        q_sample, k_sample, v_sample, g_sample, n_sample = operands
        k_blocks = k_sample.reshape(PATCHES, PATCH, D)
        v_blocks = v_sample.reshape(PATCHES, PATCH, D)

        def patch_step(running, patch_id):
            grad_k_all, grad_v_all, w_term = running
            listed = n_sample[patch_id]
            in_use = listed != patch_id
            block_ids = jnp.concatenate([patch_id[None], jnp.where(in_use, listed, patch_id)]).astype(jnp.int32)
            block_live = jnp.concatenate([jnp.array([True]), in_use])
            key_mask = jnp.repeat(block_live, PATCH)
            start = (patch_id * PATCH).astype(jnp.int32)
            q_rows = lax.dynamic_slice_in_dim(q_sample, start, PATCH, 0)
            g_rows = lax.dynamic_slice_in_dim(g_sample, start, PATCH, 0)
            key_block = k_blocks[block_ids].reshape(-1, D)
            value_block = v_blocks[block_ids].reshape(-1, D)
            attn_rows, log_total = attend(q_rows, key_block, value_block, key_mask, score_scale)
            projected = jnp.dot(attn_rows, w_out, preferred_element_type=jnp.float32).astype(jnp.bfloat16)
            d_attn = jnp.dot(g_rows, w_out.T, preferred_element_type=jnp.float32).astype(jnp.bfloat16)
            w_term = w_term + lax.dot_general(attn_rows, g_rows, (((0,), (0,)), ((), ())), preferred_element_type=jnp.float32)
            grad_q, grad_k, grad_v, row_delta = backprop(q_rows, key_block, value_block, d_attn, attn_rows, log_total, key_mask, score_scale, (NBR + 1) * PATCH)
            grad_k_all = grad_k_all.at[block_ids].add(rounded(grad_k.reshape(NBR + 1, PATCH, D)))
            grad_v_all = grad_v_all.at[block_ids].add(rounded(grad_v.reshape(NBR + 1, PATCH, D)))
            return ((grad_k_all, grad_v_all, w_term), (projected, grad_q))
        start_state = (jnp.zeros((PATCHES, PATCH, D), jnp.float32), jnp.zeros((PATCHES, PATCH, D), jnp.float32), jnp.zeros((D, D), jnp.float32))
        final, stacked = lax.scan(patch_step, start_state, jnp.arange(PATCHES, dtype=jnp.int32))
        grad_k_all, grad_v_all, w_term = final
        return (stacked[0].reshape(TOKENS, D), stacked[1].reshape(TOKENS, D), grad_k_all.reshape(TOKENS, D).astype(jnp.bfloat16), grad_v_all.reshape(TOKENS, D).astype(jnp.bfloat16), w_term)
    results = lax.map(one_sample, (queries, key_rows, value_rows, grad_out, neighbours))
    grad_w_out = lax.optimization_barrier(jnp.sum(results[4], axis=0)) / math.sqrt(SAMPLES * TOKENS)
    return (results[0], results[1], results[2], results[3], grad_w_out)
```

```python
import functools
import math

import jax
import jax.numpy as jnp
from jax import lax
from jax.experimental import pallas as pl
from jax.experimental.pallas import tpu as pltpu
from jax.sharding import PartitionSpec as P

HEADS = 8
NBR = 3
REACH = 3
F32 = jnp.float32
BF16 = jnp.bfloat16
VMEM_LIMIT = 56 * 1024 * 1024


def mm(a, b):
    return lax.dot_general(a, b, (((1,), (0,)), ((), ())), preferred_element_type=F32)


def halves(block):
    turned = block.T
    width = turned.shape[0] // 2
    return jnp.concatenate([turned[:width], turned[width:]], axis=1)


def beside(turned):
    rows = turned.shape[1]
    return jnp.concatenate([turned[:, : rows // 2], turned[:, rows // 2 :]], axis=0).T


def pack_kernel(q_ref, k_ref, v_ref, g_ref, w_ref, out_ref):
    rows = q_ref.shape[0]
    width = q_ref.shape[1] // HEADS
    half = rows // 2
    d_attn = lax.dot_general(
        g_ref[...], w_ref[...], (((1,), (1,)), ((), ())), preferred_element_type=F32
    ).astype(BF16)
    for h in range(HEADS):
        cols = slice(h * width, (h + 1) * width)
        out_ref[h, :rows, :] = jnp.concatenate([k_ref[:, cols], v_ref[:, cols]], axis=1)
        out_ref[h, rows : rows + half, :] = jnp.concatenate(
            [q_ref[:half, cols], q_ref[half:, cols]], axis=1
        )
        out_ref[h, rows + half :, :] = jnp.concatenate(
            [d_attn[:half, cols], d_attn[half:, cols]], axis=1
        )


def forward_kernel(first, ids_ref, x_ref, attn_ref, turned_ref, inv_ref, p_ref, s_scr, m_scr, o_scr, v_scr):
    step = pl.program_id(0)
    blocks, two_rows, two_width = x_ref.shape
    rows, width = two_rows // 2, two_width // 2
    half = rows // 2
    used = ids_ref[step, NBR + 1]

    @pl.when(step == 0)
    def _():
        for b in range(blocks):
            v_scr[b, :width, :] = x_ref[b, :rows, :].T[width:]
            v_scr[b, width:, :] = jnp.ones((v_scr.shape[1] - width, rows), BF16)

    q_turned = halves(x_ref[step + first, rows : rows + half, :]) * BF16(1.0 / math.sqrt(width))
    q_wide = jnp.concatenate([q_turned, jnp.zeros_like(q_turned)], axis=0)

    def score(e):
        s = mm(x_ref[ids_ref[step, e], :rows, :], q_wide)
        s_scr[e] = s
        top = jnp.max(s, axis=0, keepdims=True)
        m_scr[...] = top if e == 0 else jnp.maximum(m_scr[...], top)

    def mix(e):
        p = jnp.exp(s_scr[e] - m_scr[...]).astype(BF16)
        p_ref[0, e] = p
        term = mm(v_scr[ids_ref[step, e]], p)
        o_scr[...] = term if e == 0 else o_scr[...] + term

    for e in range(NBR + 1):
        if e < 2:
            score(e)
        else:
            pl.when(e < used)(functools.partial(score, e))
    for e in range(NBR + 1):
        if e < 2:
            mix(e)
        else:
            pl.when(e < used)(functools.partial(mix, e))
    inv = 1.0 / o_scr[width : width + 1, :]
    attn = (o_scr[:width, :] * inv).astype(BF16)
    turned_ref[0] = attn
    inv_ref[0] = jnp.broadcast_to(inv, inv_ref.shape[1:])
    attn_ref[0] = beside(attn)


def backward_kernel(first, ids_ref, x_ref, turned_ref, inv_ref, p_ref, out_ref, acc, dq_scr, k_scr, qz_scr, zd_scr, dp_scr):
    step = pl.program_id(0)
    blocks, two_rows, two_width = x_ref.shape
    rows, width = two_rows // 2, two_width // 2
    half = rows // 2
    used = ids_ref[step, NBR + 1]
    scale = 1.0 / math.sqrt(width)

    @pl.when(step == 0)
    def _():
        acc[...] = jnp.zeros_like(acc)
        for b in range(blocks):
            k_scr[b] = x_ref[b, :rows, :].T[:width]

    own = step + first
    q_turned = halves(x_ref[own, rows : rows + half, :])
    blank = jnp.zeros_like(q_turned)
    da = halves(x_ref[own, rows + half :, :]).astype(F32)
    inv = inv_ref[0, :1, :]
    da_inv = da * inv
    delta = jnp.sum(da_inv * turned_ref[0].astype(F32), axis=0, keepdims=True) * scale
    da_half = da_inv.astype(BF16)
    dp_scr[...] = jnp.concatenate([blank, da_half * BF16(scale)], axis=0)
    qz_scr[...] = jnp.concatenate([q_turned, blank], axis=0).T
    zd_scr[...] = jnp.concatenate([blank, da_half], axis=0).T

    def term(e):
        b = ids_ref[step, e]
        d_prob = mm(x_ref[b, :rows, :], dp_scr[...])
        p = p_ref[0, e]
        ds = (p.astype(F32) * (d_prob - delta)).astype(BF16)
        dq = mm(k_scr[b], ds)
        dq_scr[...] = dq if e == 0 else dq_scr[...] + dq
        acc[b] += mm(ds, qz_scr[...]) + mm(p, zd_scr[...])

    for e in range(NBR + 1):
        if e < 2:
            term(e)
        else:
            pl.when(e < used)(functools.partial(term, e))
    out_ref[own, rows:, :] = beside(dq_scr[...].astype(BF16))

    @pl.when(step == pl.num_programs(0) - 1)
    def _():
        for b in range(blocks):
            out_ref[b, :rows, :] = acc[b].astype(BF16)


def project_kernel(a_ref, g_ref, w_ref, out_ref, term_ref):
    left = jnp.concatenate([a_ref[h, :, : a_ref.shape[2] // 2] for h in range(HEADS)], axis=1)
    right = jnp.concatenate([a_ref[h, :, a_ref.shape[2] // 2 :] for h in range(HEADS)], axis=1)
    attn = jnp.concatenate([left, right], axis=0)
    out_ref[...] = mm(attn, w_ref[...]).astype(BF16)
    term_ref[...] = lax.dot_general(
        attn, g_ref[...], (((0,), (0,)), ((), ())), preferred_element_type=F32
    ).astype(BF16)


def unpack_kernel(y_ref, dq_ref, dk_ref, dv_ref):
    rows = dq_ref.shape[0]
    half = rows // 2
    width = dq_ref.shape[1] // HEADS
    for h in range(HEADS):
        cols = slice(h * width, (h + 1) * width)
        dk_ref[:, cols] = y_ref[h, :rows, :width]
        dv_ref[:, cols] = y_ref[h, :rows, width:]
        dq_ref[:half, cols] = y_ref[h, rows:, :width]
        dq_ref[half:, cols] = y_ref[h, rows:, width:]


def params():
    return pltpu.CompilerParams(vmem_limit_bytes=VMEM_LIMIT)


def cost(flops, bytes_accessed, exps=0):
    return pl.CostEstimate(flops=flops, bytes_accessed=bytes_accessed, transcendentals=exps)


def body(queries, key_rows, value_rows, w_out, grad_out, neighbours):
    _, rows, model = queries.shape
    width = model // HEADS
    half = rows // 2
    seg = lax.axis_size("seg")
    samples = lax.axis_size("sample")
    groups = seg // HEADS
    split = [[g * HEADS + i for i in range(HEADS)] for g in range(groups)] if groups > 1 else None
    halo = REACH if groups > 1 else 0
    blocks = HEADS + 2 * halo

    def swap(array):
        return lax.all_to_all(array, "seg", 0, 0, axis_index_groups=split)

    def shifted(array, by):
        pairs = [(s, s + by) for s in range(seg) if 0 <= s + by < seg]
        return lax.ppermute(array, "seg", pairs)

    listed = lax.all_gather(neighbours[0, 0], "seg", axis_index_groups=split)
    base = lax.axis_index("seg") // HEADS * HEADS
    owner = base + jnp.arange(HEADS, dtype=jnp.int32)[:, None]
    in_use = listed != owner
    ids = jnp.where(in_use, listed, owner) - base + halo
    ids = jnp.concatenate(
        [
            owner - base + halo,
            ids,
            1 + jnp.sum(in_use.astype(jnp.int32), axis=1, keepdims=True),
        ],
        axis=1,
    )

    packed = pl.pallas_call(
        pack_kernel,
        out_shape=jax.ShapeDtypeStruct((HEADS, 2 * rows, 2 * width), BF16),
        compiler_params=params(),
        cost_estimate=cost(2 * rows * model * model, 10 * rows * model),
        name="pack",
    )(queries[0], key_rows[0], value_rows[0], grad_out[0], w_out)
    x = swap(packed)
    if halo:
        x = jnp.concatenate([shifted(x[-halo:], HEADS), x, shifted(x[:halo], -HEADS)], axis=0)

    whole = lambda shape: pl.BlockSpec(shape, lambda i, ids: (0,) * len(shape))
    each = lambda shape: pl.BlockSpec((1,) + shape, lambda i, ids: (i,) + (0,) * len(shape))
    ones = 16
    units = HEADS * (NBR + 1)
    attn_out, attn_turned, inverse, probs = pl.pallas_call(
        functools.partial(forward_kernel, halo),
        grid_spec=pltpu.PrefetchScalarGridSpec(
            num_scalar_prefetch=1,
            grid=(HEADS,),
            in_specs=[whole(x.shape)],
            out_specs=[
                each((half, 2 * width)),
                each((width, rows)),
                each((8, rows)),
                each((NBR + 1, rows, rows)),
            ],
            scratch_shapes=[
                pltpu.VMEM((NBR + 1, rows, rows), F32),
                pltpu.VMEM((1, rows), F32),
                pltpu.VMEM((width + ones, rows), F32),
                pltpu.VMEM((blocks, width + ones, rows), BF16),
            ],
        ),
        out_shape=[
            jax.ShapeDtypeStruct((HEADS, half, 2 * width), BF16),
            jax.ShapeDtypeStruct((HEADS, width, rows), BF16),
            jax.ShapeDtypeStruct((HEADS, 8, rows), F32),
            jax.ShapeDtypeStruct((HEADS, NBR + 1, rows, rows), BF16),
        ],
        compiler_params=params(),
        cost_estimate=cost(units * rows * rows * 512, 20 * 2**20, units * rows * rows),
        name="forward",
    )(ids, x)
    attn_home = swap(attn_out)

    grads = pl.pallas_call(
        functools.partial(backward_kernel, halo),
        grid_spec=pltpu.PrefetchScalarGridSpec(
            num_scalar_prefetch=1,
            grid=(HEADS,),
            in_specs=[
                whole(x.shape),
                each((width, rows)),
                each((8, rows)),
                each((NBR + 1, rows, rows)),
            ],
            out_specs=whole((blocks, rows + half, 2 * width)),
            scratch_shapes=[
                pltpu.VMEM((blocks, rows, 2 * width), F32),
                pltpu.VMEM((width, rows), F32),
                pltpu.VMEM((blocks, width, rows), BF16),
                pltpu.VMEM((rows, 2 * width), BF16),
                pltpu.VMEM((rows, 2 * width), BF16),
                pltpu.VMEM((2 * width, rows), BF16),
            ],
        ),
        out_shape=jax.ShapeDtypeStruct((blocks, rows + half, 2 * width), BF16),
        compiler_params=params(),
        cost_estimate=cost(units * rows * rows * 1024, 20 * 2**20),
        name="backward",
    )(ids, x, attn_turned, inverse, probs)
    if halo:
        kv_terms = grads[:, :rows].astype(F32)
        inner = kv_terms[halo:-halo]
        inner = inner.at[-halo:].add(shifted(grads[:halo, :rows], -HEADS).astype(F32))
        inner = inner.at[:halo].add(shifted(grads[-halo:, :rows], HEADS).astype(F32))
        grads = jnp.concatenate([inner.astype(BF16), grads[halo:-halo, rows:]], axis=1)
    grads_home = swap(grads)

    attended, w_term = pl.pallas_call(
        project_kernel,
        out_shape=[
            jax.ShapeDtypeStruct((rows, model), BF16),
            jax.ShapeDtypeStruct((model, model), BF16),
        ],
        compiler_params=params(),
        cost_estimate=cost(4 * rows * model * model, 10 * rows * model),
        name="project",
    )(attn_home, grad_out[0], w_out)
    part = model // samples
    piece = part // seg
    w_part = lax.all_to_all(w_term.reshape(samples, part, model), "sample", 0, 0)
    w_part = jnp.sum(w_part.astype(F32), axis=0).astype(BF16)
    w_piece = lax.all_to_all(w_part.reshape(seg, piece, model), "seg", 0, 0)
    grad_scale = 1.0 / math.sqrt(samples * rows * seg)
    w_piece = (jnp.sum(w_piece.astype(F32), axis=0) * grad_scale).astype(BF16)
    w_part = lax.all_to_all(jnp.broadcast_to(w_piece, (seg, piece, model)), "seg", 0, 0)
    w_part = w_part.reshape(part, model)
    w_all = lax.all_to_all(jnp.broadcast_to(w_part, (samples, part, model)), "sample", 0, 0)
    grad_w_out = w_all.reshape(model, model).astype(F32)

    grad_q, grad_k, grad_v = pl.pallas_call(
        unpack_kernel,
        out_shape=[jax.ShapeDtypeStruct((rows, model), BF16)] * 3,
        compiler_params=params(),
        cost_estimate=cost(0, 12 * rows * model),
        name="unpack",
    )(grads_home)
    return attended[None], grad_q[None], grad_k[None], grad_v[None], grad_w_out


def solution(mesh):
    rows = P("sample", "seg", None)
    return jax.shard_map(
        body,
        mesh=mesh,
        in_specs=(rows, rows, rows, P(), rows, rows),
        out_specs=(rows, rows, rows, rows, P()),
        check_vma=False,
    )
```

```python
import functools
import math

import jax
import jax.numpy as jnp
from jax import lax
from jax.experimental import pallas as pl
from jax.experimental.pallas import tpu as pltpu
from jax.sharding import PartitionSpec as P

HEADS = 8
NBR = 3
REACH = 3
F32 = jnp.float32
BF16 = jnp.bfloat16
VMEM_LIMIT = 56 * 1024 * 1024


def mm(a, b):
    return lax.dot_general(a, b, (((1,), (0,)), ((), ())), preferred_element_type=F32)


def halves(block):
    turned = block.T
    width = turned.shape[0] // 2
    return jnp.concatenate([turned[:width], turned[width:]], axis=1)


def beside(turned):
    rows = turned.shape[1]
    return jnp.concatenate([turned[:, : rows // 2], turned[:, rows // 2 :]], axis=0).T


def pack_kernel(near_ref, q_ref, k_ref, v_ref, g_ref, w_ref, out_ref, d_ref):
    rows = q_ref.shape[0]
    width = q_ref.shape[1] // HEADS
    half = rows // 2
    here = lax.axis_index("seg")
    line = lax.broadcasted_iota(jnp.int32, (16, 2 * width), 0)
    offsets = jnp.zeros((16, 2 * width), F32)
    for e in range(NBR):
        offsets = jnp.where(line == e, (near_ref[0, e] - here + REACH).astype(F32), offsets)
    for h in range(HEADS):
        cols = slice(h * width, (h + 1) * width)
        out_ref[h, :rows, :] = jnp.concatenate([k_ref[:, cols], v_ref[:, cols]], axis=1)
        out_ref[h, rows : rows + half, :] = jnp.concatenate(
            [q_ref[:half, cols], q_ref[half:, cols]], axis=1
        )
        out_ref[h, rows + half :, :] = offsets.astype(BF16)
    d_attn = lax.dot_general(
        g_ref[...], w_ref[...], (((1,), (1,)), ((), ())), preferred_element_type=F32
    ).astype(BF16)
    for h in range(HEADS):
        cols = slice(h * width, (h + 1) * width)
        d_ref[h] = jnp.concatenate([d_attn[:half, cols], d_attn[half:, cols]], axis=1)


def list_units(first, near_ref, patch_of, block_of):
    count = jnp.int32(0)
    for p in range(HEADS):
        patch_of[count] = p
        block_of[count] = p + first
        count = count + 1
        for e in range(NBR):
            offset = near_ref[p, e] - REACH
            patch_of[count] = p
            block_of[count] = p + first + offset
            count = count + jnp.where(offset != 0, 1, 0)
    patch_of[count] = -1


def is_first(patch_of, u):
    return jnp.logical_or(u == 0, patch_of[jnp.maximum(u - 1, 0)] != patch_of[u])


def in_turn(step, total, one, two):
    for slot in range(2):
        mine = step % 2 == slot

        @pl.when(jnp.logical_and(mine, step == 0))
        def _():
            one(step, slot)

        @pl.when(jnp.logical_and(mine, jnp.logical_and(step > 0, step < total)))
        def _():
            two(step - 1, 1 - slot, lambda: one(step, slot))

        @pl.when(jnp.logical_and(mine, step == total))
        def _():
            two(step - 1, 1 - slot, lambda: None)


def forward_kernel(first, near_ref, x_ref, attn_ref, turned_ref, stat_ref, top_ref, p_ref, s0, s1, m_scr, o_scr, v_scr, q_scr, patch_of, block_of):
    step = pl.program_id(0)
    total = near_ref[0, NBR]
    blocks = x_ref.shape[0]
    rows, width = s0.shape[0], x_ref.shape[2] // 2
    half = rows // 2
    scores = (s0, s1)

    @pl.when(step == 0)
    def _():
        list_units(first, near_ref, patch_of, block_of)
        o_scr[...] = jnp.zeros_like(o_scr)
        for b in range(blocks):
            v_scr[b, :width, :] = x_ref[b, :rows, :].T[width:]
            v_scr[b, width:, :] = jnp.ones((v_scr.shape[1] - width, rows), BF16)
        for p in range(HEADS):
            turned = halves(x_ref[p + first, rows : rows + half, :])
            q_scr[p, :width, :] = turned * BF16(1.0 / math.sqrt(width))
            q_scr[p, width:, :] = jnp.zeros_like(turned)

    def score(u, slot):
        s = mm(x_ref[block_of[u], :rows, :], q_scr[patch_of[u]])
        scores[slot][...] = s
        top = jnp.max(s, axis=0, keepdims=True)
        top = jnp.where(is_first(patch_of, u), top, jnp.maximum(top, m_scr[...]))
        m_scr[...] = top
        top_ref[u] = top

    def mix(u, slot, then):
        m = top_ref[u]
        p = jnp.exp(scores[slot][...] - m).astype(BF16)
        p_ref[0] = p
        keep = jnp.exp(top_ref[jnp.maximum(u - 1, 0)] - m)
        keep = jnp.where(is_first(patch_of, u), 0.0, keep)
        then()
        o_scr[...] = o_scr[...] * keep + mm(v_scr[block_of[u]], p)

    in_turn(step, total, score, mix)

    u = jnp.maximum(step - 1, 0)
    ended = jnp.logical_and(step > 0, step <= total)

    @pl.when(jnp.logical_and(ended, patch_of[u + 1] != patch_of[u]))
    def _():
        p = patch_of[u]
        inv = 1.0 / o_scr[width : width + 1, :]
        attn = (o_scr[:width, :] * inv).astype(BF16)
        turned_ref[p] = attn
        stat_ref[p] = jnp.concatenate([inv, top_ref[u]], axis=0)
        attn_ref[p] = beside(attn)


def backward_kernel(first, near_ref, x_ref, d_ref, turned_ref, stat_ref, top_ref, p_ref, out_ref, acc, dp0, dp1, z0, z1, e0, e1, dq_scr, k_scr, qz_scr, d_scr, delta_scr, patch_of, block_of):
    step = pl.program_id(0)
    total = near_ref[0, NBR]
    blocks = x_ref.shape[0]
    rows, width = dp0.shape[0], x_ref.shape[2] // 2
    half = rows // 2
    scale = 1.0 / math.sqrt(width)
    d_probs, d_rows, shifts = (dp0, dp1), (z0, z1), (e0, e1)

    @pl.when(step == 0)
    def _():
        list_units(first, near_ref, patch_of, block_of)
        acc[...] = jnp.zeros_like(acc)
        dq_scr[...] = jnp.zeros_like(dq_scr)
        for b in range(blocks):
            k_scr[b] = x_ref[b, :rows, :].T[:width]
        blank = jnp.zeros((half, width), BF16)
        for p in range(HEADS):
            pair = x_ref[p + first, rows : rows + half, :]
            qz_scr[p, :half, :] = jnp.concatenate([pair[:, :width], blank], axis=1)
            qz_scr[p, half:, :] = jnp.concatenate([pair[:, width:], blank], axis=1)
            turned = halves(d_ref[p]).astype(F32)
            d_scr[p] = turned
            delta_scr[p] = jnp.sum(turned * turned_ref[p].astype(F32), axis=0, keepdims=True)

    def enter(u, slot):
        p = patch_of[u]
        share = jnp.exp(top_ref[u] - stat_ref[p, 1:2, :]) * stat_ref[p, 0:1, :]
        mine = (d_scr[p] * share).astype(BF16)
        blank = jnp.zeros_like(mine)
        d_probs[slot][...] = mm(
            x_ref[block_of[u], :rows, :],
            jnp.concatenate([blank, mine * BF16(scale)], axis=0),
        )
        shifts[slot][...] = delta_scr[p] * share * scale
        d_rows[slot][...] = jnp.concatenate([blank, mine], axis=0).T

    def leave(u, slot, then):
        b, p = block_of[u], patch_of[u]
        prob = p_ref[0]
        ds = (prob.astype(F32) * (d_probs[slot][...] - shifts[slot][...])).astype(BF16)
        then()
        dq = mm(k_scr[b], ds)
        dq_scr[...] = dq + jnp.where(is_first(patch_of, u), 0.0, dq_scr[...])
        acc[b] += mm(
            jnp.concatenate([ds, prob], axis=1),
            jnp.concatenate([qz_scr[p], d_rows[slot][...]], axis=0),
        )

    in_turn(step, total, enter, leave)

    u = jnp.maximum(step - 1, 0)
    ended = jnp.logical_and(step > 0, step <= total)

    @pl.when(jnp.logical_and(ended, patch_of[u + 1] != patch_of[u]))
    def _():
        out_ref[patch_of[u] + first, rows:, :] = beside(dq_scr[...].astype(BF16))

    @pl.when(step == total)
    def _():
        for b in range(blocks):
            out_ref[b, :rows, :] = acc[b].astype(BF16)


def project_kernel(a_ref, g_ref, w_ref, out_ref, term_ref):
    left = jnp.concatenate([a_ref[h, :, : a_ref.shape[2] // 2] for h in range(HEADS)], axis=1)
    right = jnp.concatenate([a_ref[h, :, a_ref.shape[2] // 2 :] for h in range(HEADS)], axis=1)
    attn = jnp.concatenate([left, right], axis=0)
    out_ref[...] = mm(attn, w_ref[...]).astype(BF16)
    term_ref[...] = lax.dot_general(
        attn, g_ref[...], (((0,), (0,)), ((), ())), preferred_element_type=F32
    ).astype(BF16)


def unpack_kernel(y_ref, dq_ref, dk_ref, dv_ref):
    rows = dq_ref.shape[0]
    half = rows // 2
    width = dq_ref.shape[1] // HEADS
    for h in range(HEADS):
        cols = slice(h * width, (h + 1) * width)
        dk_ref[:, cols] = y_ref[h, :rows, :width]
        dv_ref[:, cols] = y_ref[h, :rows, width:]
        dq_ref[:half, cols] = y_ref[h, rows:, :width]
        dq_ref[half:, cols] = y_ref[h, rows:, width:]


def params():
    return pltpu.CompilerParams(vmem_limit_bytes=VMEM_LIMIT)


def cost(flops, bytes_accessed, exps=0):
    return pl.CostEstimate(flops=flops, bytes_accessed=bytes_accessed, transcendentals=exps)


def body(queries, key_rows, value_rows, w_out, grad_out, neighbours):
    _, rows, model = queries.shape
    width = model // HEADS
    half = rows // 2
    seg = lax.axis_size("seg")
    samples = lax.axis_size("sample")
    groups = seg // HEADS
    split = [[g * HEADS + i for i in range(HEADS)] for g in range(groups)] if groups > 1 else None
    halo = REACH if groups > 1 else 0
    blocks = HEADS + 2 * halo

    def swap(array):
        return lax.all_to_all(array, "seg", 0, 0, axis_index_groups=split)

    def shifted(array, by):
        pairs = [(s, s + by) for s in range(seg) if 0 <= s + by < seg]
        return lax.ppermute(array, "seg", pairs)

    packed, packed_d = pl.pallas_call(
        pack_kernel,
        in_specs=[pl.BlockSpec(memory_space=pltpu.SMEM)]
        + [pl.BlockSpec(memory_space=pltpu.VMEM)] * 5,
        out_shape=[
            jax.ShapeDtypeStruct((HEADS, rows + half + 16, 2 * width), BF16),
            jax.ShapeDtypeStruct((HEADS, half, 2 * width), BF16),
        ],
        compiler_params=params(),
        cost_estimate=cost(2 * rows * model * model, 10 * rows * model),
        name="pack",
    )(neighbours[0], queries[0], key_rows[0], value_rows[0], grad_out[0], w_out)
    x = swap(packed)
    near = x[:, rows + half : rows + half + NBR, 0].astype(jnp.int32)
    total = HEADS + jnp.sum((near != REACH).astype(jnp.int32))
    near = jnp.concatenate([near, jnp.broadcast_to(total, (HEADS, 1))], axis=1)
    x, near, packed_d = lax.optimization_barrier((x, near, packed_d))
    d = swap(packed_d)
    if halo:
        x = jnp.concatenate([shifted(x[-halo:], HEADS), x, shifted(x[:halo], -HEADS)], axis=0)

    ones = 16
    units = HEADS * (NBR + 1)
    whole = lambda *shape: pl.BlockSpec(shape, lambda t, near: (0,) * len(shape))
    unit = pl.BlockSpec(
        (1, rows, rows), lambda t, near: (jnp.clip(t - 1, 0, near[0, NBR] - 1), 0, 0)
    )
    lists = [pltpu.SMEM((units + 8,), jnp.int32)] * 2
    attn_out, attn_turned, stats, tops, probs = pl.pallas_call(
        functools.partial(forward_kernel, halo),
        grid_spec=pltpu.PrefetchScalarGridSpec(
            num_scalar_prefetch=1,
            grid=(units + 1,),
            in_specs=[whole(*x.shape)],
            out_specs=[
                whole(HEADS, half, 2 * width),
                whole(HEADS, width, rows),
                whole(HEADS, 2, rows),
                whole(units, 1, rows),
                unit,
            ],
            scratch_shapes=[
                pltpu.VMEM((rows, rows), F32),
                pltpu.VMEM((rows, rows), F32),
                pltpu.VMEM((1, rows), F32),
                pltpu.VMEM((width + ones, rows), F32),
                pltpu.VMEM((blocks, width + ones, rows), BF16),
                pltpu.VMEM((HEADS, 2 * width, rows), BF16),
            ]
            + lists,
        ),
        out_shape=[
            jax.ShapeDtypeStruct((HEADS, half, 2 * width), BF16),
            jax.ShapeDtypeStruct((HEADS, width, rows), BF16),
            jax.ShapeDtypeStruct((HEADS, 2, rows), F32),
            jax.ShapeDtypeStruct((units, 1, rows), F32),
            jax.ShapeDtypeStruct((units, rows, rows), BF16),
        ],
        compiler_params=params(),
        cost_estimate=cost(units * rows * rows * 512, 20 * 2**20, units * rows * rows),
        name="forward",
    )(near, x)
    attn_home = swap(attn_out)

    grads = pl.pallas_call(
        functools.partial(backward_kernel, halo),
        grid_spec=pltpu.PrefetchScalarGridSpec(
            num_scalar_prefetch=1,
            grid=(units + 1,),
            in_specs=[
                whole(*x.shape),
                whole(HEADS, half, 2 * width),
                whole(HEADS, width, rows),
                whole(HEADS, 2, rows),
                whole(units, 1, rows),
                unit,
            ],
            out_specs=whole(blocks, rows + half, 2 * width),
            scratch_shapes=[
                pltpu.VMEM((blocks, rows, 2 * width), F32),
                pltpu.VMEM((rows, rows), F32),
                pltpu.VMEM((rows, rows), F32),
                pltpu.VMEM((rows, 2 * width), BF16),
                pltpu.VMEM((rows, 2 * width), BF16),
                pltpu.VMEM((1, rows), F32),
                pltpu.VMEM((1, rows), F32),
                pltpu.VMEM((width, rows), F32),
                pltpu.VMEM((blocks, width, rows), BF16),
                pltpu.VMEM((HEADS, rows, 2 * width), BF16),
                pltpu.VMEM((HEADS, width, rows), F32),
                pltpu.VMEM((HEADS, 1, rows), F32),
            ]
            + lists,
        ),
        out_shape=jax.ShapeDtypeStruct((blocks, rows + half, 2 * width), BF16),
        compiler_params=params(),
        cost_estimate=cost(units * rows * rows * 1024, 20 * 2**20),
        name="backward",
    )(near, x, d, attn_turned, stats, tops, probs)
    grads, attn_home = lax.optimization_barrier((grads, attn_home))
    if halo:
        kv_terms = grads[:, :rows].astype(F32)
        inner = kv_terms[halo:-halo]
        inner = inner.at[-halo:].add(shifted(grads[:halo, :rows], -HEADS).astype(F32))
        inner = inner.at[:halo].add(shifted(grads[-halo:, :rows], HEADS).astype(F32))
        grads = jnp.concatenate([inner.astype(BF16), grads[halo:-halo, rows:]], axis=1)
    grads_home = swap(grads)

    attended, w_term = pl.pallas_call(
        project_kernel,
        out_shape=[
            jax.ShapeDtypeStruct((rows, model), BF16),
            jax.ShapeDtypeStruct((model, model), BF16),
        ],
        compiler_params=params(),
        cost_estimate=cost(4 * rows * model * model, 10 * rows * model),
        name="project",
    )(attn_home, grad_out[0], w_out)
    part = model // samples
    piece = part // seg
    w_part = lax.all_to_all(w_term.reshape(samples, part, model), "sample", 0, 0)
    w_part = jnp.sum(w_part.astype(F32), axis=0).astype(BF16)
    w_piece = lax.all_to_all(w_part.reshape(seg, piece, model), "seg", 0, 0)
    grad_scale = 1.0 / math.sqrt(samples * rows * seg)
    w_piece = (jnp.sum(w_piece.astype(F32), axis=0) * grad_scale).astype(BF16)
    w_part = lax.all_to_all(jnp.broadcast_to(w_piece, (seg, piece, model)), "seg", 0, 0)
    w_part = w_part.reshape(part, model)
    w_all = lax.all_to_all(jnp.broadcast_to(w_part, (samples, part, model)), "sample", 0, 0)
    grad_w_out = w_all.reshape(model, model).astype(F32)

    grad_q, grad_k, grad_v = pl.pallas_call(
        unpack_kernel,
        out_shape=[jax.ShapeDtypeStruct((rows, model), BF16)] * 3,
        compiler_params=params(),
        cost_estimate=cost(0, 12 * rows * model),
        name="unpack",
    )(grads_home)
    return attended[None], grad_q[None], grad_k[None], grad_v[None], grad_w_out


def solution(mesh):
    rows = P("sample", "seg", None)
    return jax.shard_map(
        body,
        mesh=mesh,
        in_specs=(rows, rows, rows, P(), rows, rows),
        out_specs=(rows, rows, rows, rows, P()),
        check_vma=False,
    )
```

```python
import functools
import math

import jax
import jax.numpy as jnp
from jax import lax
from jax.experimental import pallas as pl
from jax.experimental.pallas import tpu as pltpu
from jax.sharding import PartitionSpec as P

HEADS = 8
NBR = 3
REACH = 3
F32 = jnp.float32
BF16 = jnp.bfloat16


def mm(a, b):
    return lax.dot_general(a, b, (((1,), (0,)), ((), ())), preferred_element_type=F32)


def halves(block):
    turned = block.T
    width = turned.shape[0] // 2
    return jnp.concatenate([turned[:width], turned[width:]], axis=1)


def beside(turned):
    rows = turned.shape[1]
    return jnp.concatenate([turned[:, : rows // 2], turned[:, rows // 2 :]], axis=0).T


def pack_kernel(near_ref, *refs):
    sources, (out_ref, d_ref), held, arrived = refs[:5], refs[5:7], refs[7:12], refs[12]
    copies = [
        pltpu.make_async_copy(source, target, arrived.at[i])
        for i, (source, target) in enumerate(zip(sources, held))
    ]
    for copy in copies:
        copy.start()
    for copy in copies:
        copy.wait()
    q_ref, k_ref, v_ref, g_ref, w_ref = held
    rows = q_ref.shape[0]
    width = q_ref.shape[1] // HEADS
    half = rows // 2
    here = lax.axis_index("seg")
    line = lax.broadcasted_iota(jnp.int32, (16, 2 * width), 0)
    offsets = jnp.zeros((16, 2 * width), F32)
    for e in range(NBR):
        offsets = jnp.where(line == e, (near_ref[0, e] - here + REACH).astype(F32), offsets)
    for h in range(HEADS):
        cols = slice(h * width, (h + 1) * width)
        out_ref[h, :rows, :] = jnp.concatenate([k_ref[:, cols], v_ref[:, cols]], axis=1)
        out_ref[h, rows : rows + half, :] = jnp.concatenate(
            [q_ref[:half, cols], q_ref[half:, cols]], axis=1
        )
        out_ref[h, rows + half :, :] = offsets.astype(BF16)
    d_attn = lax.dot_general(
        g_ref[...], w_ref[...], (((1,), (1,)), ((), ())), preferred_element_type=F32
    ).astype(BF16)
    for h in range(HEADS):
        cols = slice(h * width, (h + 1) * width)
        d_ref[h] = jnp.concatenate([d_attn[:half, cols], d_attn[half:, cols]], axis=1)


def list_units(first, near_ref, patch_of, block_of):
    count = jnp.int32(0)
    for p in range(HEADS):
        patch_of[count] = p
        block_of[count] = p + first
        count = count + 1
        for e in range(NBR):
            offset = near_ref[p, e] - REACH
            patch_of[count] = p
            block_of[count] = p + first + offset
            count = count + jnp.where(offset != 0, 1, 0)
    patch_of[count] = -1
    return count


def is_first(patch_of, u):
    return jnp.logical_or(u == 0, patch_of[jnp.maximum(u - 1, 0)] != patch_of[u])


def in_turn(total, patch_of, enter, leave, end):
    def both(u, slot):
        leave(u, slot, lambda: enter(u + 1, 1 - slot))
        pl.when(patch_of[u + 1] != patch_of[u])(lambda: end(u))

    def two(i, carry):
        both(2 * i, 0)
        both(2 * i + 1, 1)
        return carry

    enter(jnp.int32(0), 0)
    lax.fori_loop(0, (total - 1) // 2, two, 0)
    pl.when(total % 2 == 0)(lambda: both(total - 2, 0))
    for slot in range(2):

        @pl.when((total - 1) % 2 == slot)
        def _():
            leave(total - 1, slot, lambda: None)

    end(total - 1)


def forward_kernel(first, near_ref, x_ref, attn_ref, turned_ref, lse_ref, s0, s1, top_scr, m_scr, o_scr, v_scr, q_scr, patch_of, block_of):
    blocks = x_ref.shape[0]
    rows, width = s0.shape[0], x_ref.shape[2] // 2
    half = rows // 2
    scores = (s0, s1)
    total = list_units(first, near_ref, patch_of, block_of)
    o_scr[...] = jnp.zeros_like(o_scr)
    for b in range(blocks):
        v_scr[b, :width, :] = x_ref[b, :rows, :].T[width:]
        v_scr[b, width:, :] = jnp.ones((v_scr.shape[1] - width, rows), BF16)
    for p in range(HEADS):
        turned = halves(x_ref[p + first, rows : rows + half, :])
        q_scr[p, :width, :] = turned * BF16(1.0 / math.sqrt(width))
        q_scr[p, width:, :] = jnp.zeros_like(turned)

    def enter(u, slot):
        s = mm(x_ref[block_of[u], :rows, :], q_scr[patch_of[u]])
        scores[slot][...] = s
        top = jnp.max(s, axis=0, keepdims=True)
        top = jnp.where(is_first(patch_of, u), top, jnp.maximum(top, m_scr[...]))
        m_scr[...] = top
        top_scr[u] = top

    def leave(u, slot, then):
        m = top_scr[u]
        p = jnp.exp(scores[slot][...] - m).astype(BF16)
        keep = jnp.exp(top_scr[jnp.maximum(u - 1, 0)] - m)
        keep = jnp.where(is_first(patch_of, u), 0.0, keep)
        then()
        o_scr[...] = o_scr[...] * keep + mm(v_scr[block_of[u]], p)

    def end(u):
        p = patch_of[u]
        total_p = o_scr[width : width + 1, :]
        attn = (o_scr[:width, :] * (1.0 / total_p)).astype(BF16)
        turned_ref[p] = attn
        lse_ref[p] = top_scr[u] + jnp.log(total_p)
        attn_ref[p] = beside(attn)

    in_turn(total, patch_of, enter, leave, end)


def backward_kernel(first, near_ref, x_ref, d_ref, turned_ref, lse_ref, out_ref, acc, s0, s1, dq_scr, k_scr, back_scr, q_scr, d_scr, delta_scr, patch_of, block_of):
    blocks = x_ref.shape[0]
    rows, width = q_scr.shape[2], x_ref.shape[2] // 2
    half = rows // 2
    scale = 1.0 / math.sqrt(width)
    pairs = (s0, s1)
    total = list_units(first, near_ref, patch_of, block_of)
    acc[...] = jnp.zeros_like(acc)
    dq_scr[...] = jnp.zeros_like(dq_scr)
    for b in range(blocks):
        k_scr[b] = x_ref[b, :rows, :].T[:width]
    blank = jnp.zeros((half, width), BF16)
    for p in range(HEADS):
        q_pair = x_ref[p + first, rows : rows + half, :]
        d_pair = d_ref[p]
        back_scr[p, :half, :] = jnp.concatenate([q_pair[:, :width], blank], axis=1)
        back_scr[p, half:rows, :] = jnp.concatenate([q_pair[:, width:], blank], axis=1)
        back_scr[p, rows : rows + half, :] = jnp.concatenate([blank, d_pair[:, :width]], axis=1)
        back_scr[p, rows + half :, :] = jnp.concatenate([blank, d_pair[:, width:]], axis=1)
        q_turned, d_turned = halves(q_pair), halves(d_pair)
        q_scr[p, :width, :] = q_turned * BF16(scale)
        q_scr[p, width:, :] = jnp.zeros_like(q_turned)
        d_scr[p, :width, :] = jnp.zeros_like(d_turned)
        d_scr[p, width:, :] = d_turned * BF16(scale)
        product = d_turned.astype(F32) * turned_ref[p].astype(F32)
        delta_scr[p] = jnp.sum(product, axis=0, keepdims=True) * scale

    def enter(u, slot):
        keys, p = x_ref[block_of[u], :rows, :], patch_of[u]
        pairs[slot][:, :rows] = mm(keys, q_scr[p])
        pairs[slot][:, rows:] = mm(keys, d_scr[p])

    def leave(u, slot, then):
        b, p = block_of[u], patch_of[u]
        prob = jnp.exp(pairs[slot][:, :rows] - lse_ref[p])
        ds = (prob * (pairs[slot][:, rows:] - delta_scr[p])).astype(BF16)
        then()
        dq = mm(k_scr[b], ds)
        dq_scr[...] = dq + jnp.where(is_first(patch_of, u), 0.0, dq_scr[...])
        acc[b] += mm(jnp.concatenate([ds, prob.astype(BF16)], axis=1), back_scr[p])

    def end(u):
        out_ref[patch_of[u] + first, rows:, :] = beside(dq_scr[...].astype(BF16))

    in_turn(total, patch_of, enter, leave, end)
    for b in range(blocks):
        out_ref[b, :rows, :] = acc[b].astype(BF16)


def project_kernel(a_ref, g_ref, w_ref, out_ref, term_ref):
    left = jnp.concatenate([a_ref[h, :, : a_ref.shape[2] // 2] for h in range(HEADS)], axis=1)
    right = jnp.concatenate([a_ref[h, :, a_ref.shape[2] // 2 :] for h in range(HEADS)], axis=1)
    attn = jnp.concatenate([left, right], axis=0)
    out_ref[...] = mm(attn, w_ref[...]).astype(BF16)
    term_ref[...] = lax.dot_general(
        attn, g_ref[...], (((0,), (0,)), ((), ())), preferred_element_type=F32
    ).astype(BF16)


def unpack_kernel(y_ref, dq_ref, dk_ref, dv_ref):
    rows = dq_ref.shape[0]
    half = rows // 2
    width = dq_ref.shape[1] // HEADS
    for h in range(HEADS):
        cols = slice(h * width, (h + 1) * width)
        dk_ref[:, cols] = y_ref[h, :rows, :width]
        dv_ref[:, cols] = y_ref[h, :rows, width:]
        dq_ref[:half, cols] = y_ref[h, rows:, :width]
        dq_ref[half:, cols] = y_ref[h, rows:, width:]


def params(mib=32):
    return pltpu.CompilerParams(vmem_limit_bytes=mib * 2**20)


def cost(flops, bytes_accessed, exps=0):
    return pl.CostEstimate(flops=flops, bytes_accessed=bytes_accessed, transcendentals=exps)


def forward(near, x, halo):
    blocks, two_width = x.shape[0], x.shape[2]
    width = two_width // 2
    rows = (x.shape[1] - 16) * 2 // 3
    half = rows // 2
    units = HEADS * (NBR + 1)
    ones = 16
    vmem = pl.BlockSpec(memory_space=pltpu.VMEM)
    return pl.pallas_call(
        functools.partial(forward_kernel, halo),
        in_specs=[pl.BlockSpec(memory_space=pltpu.SMEM), vmem],
        out_specs=[vmem] * 3,
        scratch_shapes=[
            pltpu.VMEM((rows, rows), F32),
            pltpu.VMEM((rows, rows), F32),
            pltpu.VMEM((units, 1, rows), F32),
            pltpu.VMEM((1, rows), F32),
            pltpu.VMEM((width + ones, rows), F32),
            pltpu.VMEM((blocks, width + ones, rows), BF16),
            pltpu.VMEM((HEADS, two_width, rows), BF16),
            pltpu.SMEM((units + 8,), jnp.int32),
            pltpu.SMEM((units + 8,), jnp.int32),
        ],
        out_shape=[
            jax.ShapeDtypeStruct((HEADS, half, two_width), BF16),
            jax.ShapeDtypeStruct((HEADS, width, rows), BF16),
            jax.ShapeDtypeStruct((HEADS, 1, rows), F32),
        ],
        compiler_params=params(),
        cost_estimate=cost(units * rows * rows * 512, 4 * 2**20, units * rows * rows),
        name="forward",
    )(near, x)


def backward(near, x, d, turned, lse, halo):
    blocks, two_width = x.shape[0], x.shape[2]
    width = two_width // 2
    rows = (x.shape[1] - 16) * 2 // 3
    half = rows // 2
    units = HEADS * (NBR + 1)
    vmem = pl.BlockSpec(memory_space=pltpu.VMEM)
    return pl.pallas_call(
        functools.partial(backward_kernel, halo),
        in_specs=[pl.BlockSpec(memory_space=pltpu.SMEM)] + [vmem] * 4,
        out_specs=vmem,
        scratch_shapes=[
            pltpu.VMEM((blocks, rows, two_width), F32),
            pltpu.VMEM((rows, 2 * rows), F32),
            pltpu.VMEM((rows, 2 * rows), F32),
            pltpu.VMEM((width, rows), F32),
            pltpu.VMEM((blocks, width, rows), BF16),
            pltpu.VMEM((HEADS, 2 * rows, two_width), BF16),
            pltpu.VMEM((HEADS, two_width, rows), BF16),
            pltpu.VMEM((HEADS, two_width, rows), BF16),
            pltpu.VMEM((HEADS, 1, rows), F32),
            pltpu.SMEM((units + 8,), jnp.int32),
            pltpu.SMEM((units + 8,), jnp.int32),
        ],
        out_shape=jax.ShapeDtypeStruct((blocks, rows + half, two_width), BF16),
        compiler_params=params(),
        cost_estimate=cost(units * rows * rows * 1280, 6 * 2**20, units * rows * rows),
        name="backward",
    )(near, x, d, turned, lse)


def in_hbm(array):
    return pltpu.with_memory_space_constraint(array, pltpu.HBM)


def around(count, by):
    return [(i, (i + by) % count) for i in range(count)]


def exchange(pieces, axis):
    count = pieces.shape[0]
    if count > HEADS:
        return lax.all_to_all(pieces, axis, 0, 0)
    here = lax.axis_index(axis)
    arrived = []
    for by in range(count):
        piece = lax.dynamic_index_in_dim(pieces, (here + by) % count, 0, keepdims=False)
        arrived.append(lax.ppermute(piece, axis, around(count, by)) if by else piece)
    return jnp.stack(arrived)


def gathered(piece, axis):
    count = lax.axis_size(axis)
    if count > HEADS:
        return lax.all_gather(piece, axis)
    here = lax.axis_index(axis)
    arrived = [lax.ppermute(piece, axis, around(count, by)) if by else piece for by in range(count)]
    line = jnp.stack(arrived[::-1] + arrived[::-1])
    return lax.dynamic_slice_in_dim(line, count - 1 - here, count, 0)


def body(queries, key_rows, value_rows, w_out, grad_out, neighbours):
    _, rows, model = queries.shape
    width = model // HEADS
    half = rows // 2
    seg = lax.axis_size("seg")
    samples = lax.axis_size("sample")
    groups = seg // HEADS
    split = [[g * HEADS + i for i in range(HEADS)] for g in range(groups)] if groups > 1 else None
    halo = REACH if groups > 1 else 0
    blocks = HEADS + 2 * halo

    def swap(array):
        return lax.all_to_all(array, "seg", 0, 0, axis_index_groups=split)

    def shifted(array, by):
        pairs = [(s, s + by) for s in range(seg) if 0 <= s + by < seg]
        return lax.ppermute(array, "seg", pairs)

    packed, packed_d = pl.pallas_call(
        pack_kernel,
        in_specs=[pl.BlockSpec(memory_space=pltpu.SMEM)]
        + [pl.BlockSpec(memory_space=pltpu.HBM)] * 5,
        scratch_shapes=[pltpu.VMEM((rows, model), BF16)] * 4
        + [pltpu.VMEM((model, model), BF16), pltpu.SemaphoreType.DMA((5,))],
        out_shape=[
            jax.ShapeDtypeStruct((HEADS, rows + half + 16, 2 * width), BF16),
            jax.ShapeDtypeStruct((HEADS, half, 2 * width), BF16),
        ],
        compiler_params=params(),
        cost_estimate=cost(2 * rows * model * model, 10 * rows * model),
        name="pack",
    )(neighbours[0], *(in_hbm(a) for a in (queries[0], key_rows[0], value_rows[0], grad_out[0], w_out)))
    x = swap(packed)
    near = x[:, rows + half : rows + half + NBR, 0].astype(jnp.int32)
    x, near, packed_d = lax.optimization_barrier((x, near, packed_d))
    d = swap(packed_d)
    if halo:
        x = jnp.concatenate([shifted(x[-halo:], HEADS), x, shifted(x[:halo], -HEADS)], axis=0)

    attn_out, attn_turned, lse = forward(near, x, halo)
    attn_home = swap(attn_out)

    grads = backward(near, x, d, attn_turned, lse, halo)
    grads, attn_home = lax.optimization_barrier((grads, attn_home))
    if halo:
        kv_terms = grads[:, :rows].astype(F32)
        inner = kv_terms[halo:-halo]
        inner = inner.at[-halo:].add(shifted(grads[:halo, :rows], -HEADS).astype(F32))
        inner = inner.at[:halo].add(shifted(grads[-halo:, :rows], HEADS).astype(F32))
        grads = jnp.concatenate([inner.astype(BF16), grads[halo:-halo, rows:]], axis=1)
    grads_home = swap(grads)

    attended, w_term = pl.pallas_call(
        project_kernel,
        out_shape=[
            jax.ShapeDtypeStruct((rows, model), BF16),
            jax.ShapeDtypeStruct((model, model), BF16),
        ],
        compiler_params=params(),
        cost_estimate=cost(4 * rows * model * model, 10 * rows * model),
        name="project",
    )(attn_home, grad_out[0], w_out)
    part = model // samples
    w_part = exchange(w_term.reshape(samples, part, model), "sample")
    w_part = jnp.sum(w_part.astype(F32), axis=0).astype(BF16)
    w_piece = exchange(w_part.reshape(seg, part // seg, model), "seg")
    grad_scale = 1.0 / math.sqrt(samples * rows * seg)
    w_piece = (jnp.sum(w_piece.astype(F32), axis=0) * grad_scale).astype(BF16)
    grad_q, grad_k, grad_v = pl.pallas_call(
        unpack_kernel,
        out_shape=[jax.ShapeDtypeStruct((rows, model), BF16)] * 3,
        compiler_params=params(),
        cost_estimate=cost(0, 12 * rows * model),
        name="unpack",
    )(grads_home)
    w_piece, grad_q = lax.optimization_barrier((w_piece, grad_q))
    w_part = gathered(w_piece, "seg").reshape(part, model)
    grad_w_out = gathered(w_part, "sample").reshape(model, model).astype(F32)
    return attended[None], grad_q[None], grad_k[None], grad_v[None], grad_w_out


def solution(mesh):
    rows = P("sample", "seg", None)
    return jax.shard_map(
        body,
        mesh=mesh,
        in_specs=(rows, rows, rows, P(), rows, rows),
        out_specs=(rows, rows, rows, rows, P()),
        check_vma=False,
    )
```

```python
import functools
import math

import jax
import jax.numpy as jnp
from jax import lax
from jax.experimental import pallas as pl
from jax.experimental.pallas import tpu as pltpu
from jax.sharding import PartitionSpec as P

HEADS = 8
NBR = 3
REACH = 3
GROUP = 4
MINE = HEADS // GROUP
F32 = jnp.float32
BF16 = jnp.bfloat16


def mm(a, b):
    return lax.dot_general(a, b, (((1,), (0,)), ((), ())), preferred_element_type=F32)


def halves(block):
    turned = block.T
    width = turned.shape[0] // 2
    return jnp.concatenate([turned[:width], turned[width:]], axis=1)


def beside(turned):
    rows = turned.shape[1]
    return jnp.concatenate([turned[:, : rows // 2], turned[:, rows // 2 :]], axis=0).T


def pack_kernel(near_ref, *refs):
    sources, out_ref, held, arrived = refs[:3], refs[3], refs[4:7], refs[7]
    copies = [
        pltpu.make_async_copy(source, target, arrived.at[i])
        for i, (source, target) in enumerate(zip(sources, held))
    ]
    for copy in copies:
        copy.start()
    for copy in copies:
        copy.wait()
    q_ref, k_ref, v_ref = held
    rows = q_ref.shape[0]
    width = q_ref.shape[1] // HEADS
    half = rows // 2
    here = lax.axis_index("seg")
    line = lax.broadcasted_iota(jnp.int32, (16, 2 * width), 0)
    offsets = jnp.zeros((16, 2 * width), F32)
    for e in range(NBR):
        offsets = jnp.where(line == e, (near_ref[0, e] - here + REACH).astype(F32), offsets)
    for h in range(HEADS):
        to, i = divmod(h, MINE)
        cols = slice(h * width, (h + 1) * width)
        at_q = MINE * rows + i * half
        out_ref[to, i * rows : (i + 1) * rows, :] = jnp.concatenate(
            [k_ref[:, cols], v_ref[:, cols]], axis=1
        )
        out_ref[to, at_q : at_q + half, :] = jnp.concatenate(
            [q_ref[:half, cols], q_ref[half:, cols]], axis=1
        )
        out_ref[to, MINE * (rows + half) :, :] = offsets.astype(BF16)


def list_units(near_ref, patch_of, block_of, count, first, outside, right=0, base=0):
    for p in range(GROUP):
        if not outside:
            patch_of[count] = first + p
            block_of[count] = first + p
            count = count + 1
        for e in range(NBR):
            t = p + near_ref[p, e] - REACH
            inside = jnp.logical_and(t >= 0, t < GROUP)
            patch_of[count] = first + p
            if outside:
                want = jnp.logical_not(inside)
                block_of[count] = base + jnp.where(t < 0, t + REACH, t - GROUP + right)
            else:
                want = jnp.logical_and(inside, t != p)
                block_of[count] = first + t
            count = count + jnp.where(want, 1, 0)
    return count


def in_turn(total, enter, leave):
    def both(u, slot):
        leave(u, slot, lambda: enter(u + 1, 1 - slot))

    def two(i, carry):
        both(2 * i, 0)
        both(2 * i + 1, 1)
        return carry

    @pl.when(total > 0)
    def _():
        enter(jnp.int32(0), 0)
        lax.fori_loop(0, (total - 1) // 2, two, 0)
        pl.when(total % 2 == 0)(lambda: both(total - 2, 0))
        for slot in range(2):

            @pl.when((total - 1) % 2 == slot)
            def _():
                leave(total - 1, slot, lambda: None)


def mix_units(total, patch_of, block_of, keys, q_scr, v_scr, scores, before_scr, top_scr, m_ref, o_ref):
    def enter(u, slot):
        p = patch_of[u]
        s = mm(keys(block_of[u]), q_scr[p])
        scores[slot][...] = s
        before = m_ref[p]
        top = jnp.maximum(before, jnp.max(s, axis=0, keepdims=True))
        before_scr[u] = before
        top_scr[u] = top
        m_ref[p] = top

    def leave(u, slot, then):
        p, top = patch_of[u], top_scr[u]
        prob = jnp.exp(scores[slot][...] - top).astype(BF16)
        keep = jnp.exp(before_scr[u] - top)
        then()
        o_ref[p] = o_ref[p] * keep + mm(v_scr[block_of[u]], prob)

    in_turn(total, enter, leave)


def back_units(total, patch_of, block_of, keys, q_scr, d_scr, back_scr, k_scr, pairs, lse_ref, delta_ref, dq_ref, acc):
    rows = q_scr.shape[2]

    def enter(u, slot):
        block, p = keys(block_of[u]), patch_of[u]
        pairs[slot][:, :rows] = mm(block, q_scr[p])
        pairs[slot][:, rows:] = mm(block, d_scr[p])

    def leave(u, slot, then):
        b, p = block_of[u], patch_of[u]
        prob = jnp.exp(pairs[slot][:, :rows] - lse_ref[p])
        ds = (prob * (pairs[slot][:, rows:] - delta_ref[p])).astype(BF16)
        then()
        dq_ref[p] += mm(k_scr[b], ds)
        acc[b] += mm(jnp.concatenate([ds, prob.astype(BF16)], axis=1), back_scr[p])

    in_turn(total, enter, leave)


def fill_q(x_ref, head, rows, width, q_scr, at):
    half = rows // 2
    start = MINE * rows + head * half
    for p in range(GROUP):
        turned = halves(x_ref[p, start : start + half, :])
        q_scr[at + p, :width, :] = turned * BF16(1.0 / math.sqrt(width))
        q_scr[at + p, width:, :] = jnp.zeros_like(turned)


def fill_back(x_ref, d_ref, head, rows, width, d_scr, back_scr, at=0):
    half = rows // 2
    start = MINE * rows + head * half
    blank = jnp.zeros((half, width), BF16)
    for p in range(GROUP):
        q_pair = x_ref[p, start : start + half, :]
        d_pair = d_ref[p, head * half : (head + 1) * half, :]
        back_scr[at + p, :half, :] = jnp.concatenate([q_pair[:, :width], blank], axis=1)
        back_scr[at + p, half:rows, :] = jnp.concatenate([q_pair[:, width:], blank], axis=1)
        back_scr[at + p, rows : rows + half, :] = jnp.concatenate([blank, d_pair[:, :width]], axis=1)
        back_scr[at + p, rows + half :, :] = jnp.concatenate([blank, d_pair[:, width:]], axis=1)
        d_turned = halves(d_pair)
        d_scr[at + p, :width, :] = jnp.zeros_like(d_turned)
        d_scr[at + p, width:, :] = d_turned * BF16(1.0 / math.sqrt(width))


def near_kernel(near_ref, x_ref, o_ref, m_ref, s0, s1, before_scr, top_scr, q_scr, v_scr, patch_of, block_of):
    rows, width = s0.shape[0], x_ref.shape[2] // 2
    total = jnp.int32(0)
    for i in range(MINE):
        total = list_units(near_ref, patch_of, block_of, total, i * GROUP, False)
        fill_q(x_ref, i, rows, width, q_scr, i * GROUP)
        for b in range(GROUP):
            turned = x_ref[b, i * rows : (i + 1) * rows, :].T
            v_scr[i * GROUP + b, :width, :] = turned[width:]
            v_scr[i * GROUP + b, width:, :] = jnp.ones((v_scr.shape[1] - width, rows), BF16)
    o_ref[...] = jnp.zeros_like(o_ref)
    m_ref[...] = jnp.full_like(m_ref, -jnp.inf)

    def keys(b):
        return x_ref[b % GROUP, pl.ds(pl.multiple_of(b // GROUP * rows, rows), rows), :]

    mix_units(total, patch_of, block_of, keys, q_scr, v_scr, (s0, s1), before_scr, top_scr, m_ref, o_ref)


def far_kernel(right, near_ref, x_ref, g_ref, w_ref, halo_ref, o_in, m_in, attn_ref, lse_ref, delta_ref, dq_ref, d_ref, term_ref, out_ref, acc, s0, s1, before_scr, top_scr, m_scr, o_scr, q_scr, d_scr, back_scr, v_scr, k_scr, patch_of, block_of):
    rows, width = q_scr.shape[2], x_ref.shape[2] // 2
    half, halo = rows // 2, halo_ref.shape[0]
    me = lax.axis_index("seg")
    other = 1 - me // GROUP if out_ref.shape[0] == 2 else 0
    place = me % GROUP * MINE * width
    mine = w_ref[pl.ds(pl.multiple_of(place, MINE * width), MINE * width), :]
    for p in range(GROUP):
        d_attn = lax.dot_general(
            mine, g_ref[p], (((1,), (1,)), ((), ())), preferred_element_type=F32
        ).astype(BF16)
        for i in range(MINE):
            d_ref[p, i * half : (i + 1) * half, :] = beside(d_attn[i * width : (i + 1) * width])
    total = jnp.int32(0)
    for i in range(MINE):
        total = list_units(near_ref, patch_of, block_of, total, i * GROUP, True, right, i * halo)
        fill_q(x_ref, i, rows, width, q_scr, i * GROUP)
        fill_back(x_ref, d_ref, i, rows, width, d_scr, back_scr, i * GROUP)
        for b in range(halo):
            turned = halo_ref[b, i * rows : (i + 1) * rows, :].T
            k_scr[i * halo + b] = turned[:width]
            v_scr[i * halo + b, :width, :] = turned[width:]
            v_scr[i * halo + b, width:, :] = jnp.ones((v_scr.shape[1] - width, rows), BF16)
    o_scr[...] = o_in[...]
    m_scr[...] = m_in[...]

    def keys(b):
        return halo_ref[b % halo, pl.ds(pl.multiple_of(b // halo * rows, rows), rows), :]

    firsts = (s0.at[:, :rows], s1.at[:, :rows])
    mix_units(total, patch_of, block_of, keys, q_scr, v_scr, firsts, before_scr, top_scr, m_scr, o_scr)
    attns = []
    for p in range(MINE * GROUP):
        sums = o_scr[p, width : width + 1, :]
        attn = (o_scr[p, :width, :] * (1.0 / sums)).astype(BF16)
        attns.append(attn)
        attn_ref[p % GROUP, p // GROUP * half : (p // GROUP + 1) * half, :] = beside(attn)
        lse_ref[p] = m_scr[p] + jnp.log(sums)
        product = d_scr[p, width:, :].astype(F32) * attn.astype(F32)
        delta_ref[p] = jnp.sum(product, axis=0, keepdims=True)
    term = jnp.zeros(term_ref.shape, F32)
    for p in range(GROUP):
        rows_here = jnp.concatenate([attns[i * GROUP + p] for i in range(MINE)], axis=0)
        term = term + mm(rows_here, g_ref[p])
    term_ref[...] = term.astype(BF16)
    acc[...] = jnp.zeros_like(acc)
    dq_ref[...] = jnp.zeros_like(dq_ref)
    back_units(total, patch_of, block_of, keys, q_scr, d_scr, back_scr, k_scr, (s0, s1), lse_ref, delta_ref, dq_ref, acc)
    for i in range(MINE):
        for b in range(halo):
            out_ref[other, b, i * rows : (i + 1) * rows, :] = acc[i * halo + b].astype(BF16)


def own_kernel(head, near_ref, x_ref, d_ref, lse_ref, delta_ref, dq_in, out_ref, acc, s0, s1, dq_scr, q_scr, d_scr, back_scr, k_scr, patch_of, block_of):
    rows, width = q_scr.shape[2], x_ref.shape[2] // 2
    total = list_units(near_ref, patch_of, block_of, jnp.int32(0), 0, False)
    fill_q(x_ref, head, rows, width, q_scr, 0)
    fill_back(x_ref, d_ref, head, rows, width, d_scr, back_scr)
    mine = slice(head * rows, (head + 1) * rows)
    for b in range(GROUP):
        k_scr[b] = x_ref[b, mine, :].T[:width]
    own = pl.ds(head * GROUP, GROUP)
    acc[...] = jnp.zeros_like(acc)
    dq_scr[...] = dq_in[head * GROUP : (head + 1) * GROUP]
    keys = lambda b: x_ref[b, mine, :]
    back_units(total, patch_of, block_of, keys, q_scr, d_scr, back_scr, k_scr, (s0, s1), lse_ref.at[own], delta_ref.at[own], dq_scr, acc)
    for p in range(GROUP):
        out_ref[p, :rows, :] = acc[p].astype(BF16)
        out_ref[p, rows:, :] = beside(dq_scr[p].astype(BF16))


def merge_kernel(alone, *refs):
    owns, back_ref, attn_ref, out_ref = refs[:MINE], refs[MINE], refs[-2], refs[-1]
    each = owns[0].shape[1]
    rows = each * 2 // 3
    for p in range(GROUP):
        out_ref[p, MINE * each :, :] = attn_ref[p]
    for i in range(MINE):
        for p in range(GROUP):
            out_ref[p, i * each : (i + 1) * each, :] = owns[i][p]
        mine = slice(i * each, i * each + rows)
        other = 1 - lax.axis_index("seg") // GROUP if alone else 0
        for side in range(back_ref.shape[1] // REACH):
            start = other if alone else 1 - side
            for j in range(REACH):
                term = back_ref[other, side * REACH + j, i * rows : (i + 1) * rows, :].astype(F32)
                here = out_ref[start + j, mine, :].astype(F32)
                out_ref[start + j, mine, :] = (here + term).astype(BF16)


def unpack_kernel(y_ref, w_ref, out_ref, dq_ref, dk_ref, dv_ref):
    rows, width = dk_ref.shape[0], y_ref.shape[2] // 2
    half = rows // 2
    sides = ([], [])
    for h in range(HEADS):
        cols = slice(h * width, (h + 1) * width)
        r, i = divmod(h, MINE)
        at = i * (rows + half)
        dk_ref[:, cols] = y_ref[r, at : at + rows, :width]
        dv_ref[:, cols] = y_ref[r, at : at + rows, width:]
        dq_ref[:half, cols] = y_ref[r, at + rows : at + rows + half, :width]
        dq_ref[half:, cols] = y_ref[r, at + rows : at + rows + half, width:]
        at = MINE * (rows + half) + i * half
        sides[0].append(y_ref[r, at : at + half, :width])
        sides[1].append(y_ref[r, at : at + half, width:])
    attn = jnp.concatenate([jnp.concatenate(side, axis=1) for side in sides], axis=0)
    out_ref[...] = mm(attn, w_ref[...]).astype(BF16)


def params(mib=32):
    return pltpu.CompilerParams(vmem_limit_bytes=mib * 2**20)


def cost(flops, bytes_accessed, exps=0):
    return pl.CostEstimate(flops=flops // 1000, bytes_accessed=bytes_accessed // 1000, transcendentals=0)


def in_hbm(array):
    return pltpu.with_memory_space_constraint(array, pltpu.HBM)


def around(count, by):
    return [(i, (i + by) % count) for i in range(count)]


def exchange(pieces, axis):
    count = pieces.shape[0]
    if count > HEADS:
        return lax.all_to_all(pieces, axis, 0, 0)
    here = lax.axis_index(axis)
    arrived = []
    for by in range(count):
        piece = lax.dynamic_index_in_dim(pieces, (here + by) % count, 0, keepdims=False)
        arrived.append(lax.ppermute(piece, axis, around(count, by)) if by else piece)
    return jnp.stack(arrived)


def gathered(piece, axis, count):
    size = lax.axis_size(axis)
    here = lax.axis_index(axis) % count
    arrived = [piece]
    for by in range(1, count):
        pairs = [(i, i // count * count + (i + by) % count) for i in range(size)]
        arrived.append(lax.ppermute(piece, axis, pairs))
    line = jnp.stack(arrived[::-1] + arrived[::-1])
    return lax.dynamic_slice_in_dim(line, count - 1 - here, count, 0)


def body(queries, key_rows, value_rows, w_out, grad_out, neighbours):
    _, rows, model = queries.shape
    width = model // HEADS
    half, wide = rows // 2, 2 * width
    seg = lax.axis_size("seg")
    samples = lax.axis_size("sample")
    groups = seg // GROUP
    split = [[g * GROUP + i for i in range(GROUP)] for g in range(groups)]
    alone = groups == 2
    halo = REACH if alone else 2 * REACH
    ones = 16
    most = GROUP * (NBR + 1)
    vmem = pl.BlockSpec(memory_space=pltpu.VMEM)
    smem = pl.BlockSpec(memory_space=pltpu.SMEM)
    unit_cost = rows * rows

    def swap(array):
        return lax.all_to_all(array, "seg", 0, 0, axis_index_groups=split)

    def shifted(array, by):
        pairs = [(s, s + by) for s in range(seg) if 0 <= s + by < seg]
        return lax.ppermute(array, "seg", pairs)

    def across(array):
        return lax.ppermute(array, "seg", [(s, (s + GROUP) % seg) for s in range(seg)])

    def between(array):
        pairs = [[i, i + GROUP] for i in range(GROUP)]
        return lax.all_to_all(array, "seg", 0, 0, axis_index_groups=pairs)

    def call(kernel, name, outs, scratch, flops, exps=0, mib=32):
        return pl.pallas_call(
            kernel,
            out_shape=[jax.ShapeDtypeStruct(shape, kind) for shape, kind in outs],
            out_specs=[vmem] * len(outs),
            scratch_shapes=scratch,
            compiler_params=params(mib),
            cost_estimate=cost(flops, 4 * 2**20, exps),
            name=name,
        )

    packed = pl.pallas_call(
        pack_kernel,
        in_specs=[smem] + [pl.BlockSpec(memory_space=pltpu.HBM)] * 3,
        scratch_shapes=[pltpu.VMEM((rows, model), BF16)] * 3 + [pltpu.SemaphoreType.DMA((3,))],
        out_shape=jax.ShapeDtypeStruct((GROUP, MINE * (rows + half) + 16, wide), BF16),
        compiler_params=params(),
        cost_estimate=cost(2 * rows * model * model, 10 * rows * model),
        name="pack",
    )(neighbours[0], *(in_hbm(a) for a in (queries[0], key_rows[0], value_rows[0])))
    x = swap(packed)
    at = MINE * (rows + half)
    near = x[:, at : at + NBR, 0].astype(jnp.int32)
    copies = jnp.broadcast_to(grad_out, (GROUP, rows, model))
    x, near, copies = lax.optimization_barrier((x, near, copies))
    kv = x[:, : MINE * rows]
    if alone:
        first = 1 - lax.axis_index("seg") // GROUP
        beyond = lax.dynamic_slice_in_dim(kv, first, REACH, 0)
        beyond = across(beyond)
    else:
        beyond = jnp.concatenate([shifted(kv[1:], GROUP), shifted(kv[:REACH], -GROUP)], axis=0)
    grads_here = swap(copies)

    lists = lambda count: [pltpu.SMEM((count + 8,), jnp.int32)] * 2
    sheet = pltpu.VMEM((rows, rows), F32)
    double = pltpu.VMEM((rows, 2 * rows), F32)
    lines = lambda count: pltpu.VMEM((count, 1, rows), F32)
    patches = MINE * GROUP
    o_state, m_state = call(
        near_kernel,
        "near",
        [((patches, width + ones, rows), F32), ((patches, 1, rows), F32)],
        [
            sheet,
            sheet,
            lines(MINE * most),
            lines(MINE * most),
            pltpu.VMEM((patches, wide, rows), BF16),
            pltpu.VMEM((patches, width + ones, rows), BF16),
        ]
        + lists(MINE * most),
        20 * unit_cost * 512,
        20 * unit_cost,
    )(near, x)

    attn, lse, delta, dq, d, w_term, far = call(
        functools.partial(far_kernel, halo - REACH),
        "far",
        [
            ((GROUP, MINE * half, wide), BF16),
            ((patches, 1, rows), F32),
            ((patches, 1, rows), F32),
            ((patches, width, rows), F32),
            ((GROUP, MINE * half, wide), BF16),
            ((MINE * width, model), BF16),
            ((2 if alone else 1, halo, MINE * rows, wide), BF16),
        ],
        [
            pltpu.VMEM((MINE * halo, rows, wide), F32),
            double,
            double,
            lines(MINE * most),
            lines(MINE * most),
            lines(patches),
            pltpu.VMEM((patches, width + ones, rows), F32),
            pltpu.VMEM((patches, wide, rows), BF16),
            pltpu.VMEM((patches, wide, rows), BF16),
            pltpu.VMEM((patches, 2 * rows, wide), BF16),
            pltpu.VMEM((MINE * halo, width + ones, rows), BF16),
            pltpu.VMEM((MINE * halo, width, rows), BF16),
        ]
        + lists(MINE * most),
        6 * unit_cost * 1536,
        12 * unit_cost,
        60,
    )(near, x, grads_here, w_out, beyond, o_state, m_state)
    if alone:
        back = between(far)
    else:
        far = far[0]
        back = jnp.concatenate([shifted(far[:REACH], -GROUP), shifted(far[REACH:], GROUP)], axis=0)
        back = back[None]
    def own_terms(i, lse, delta, dq):
        return call(
            functools.partial(own_kernel, i),
            f"own{i}",
            [((GROUP, rows + half, wide), BF16)],
            [
                pltpu.VMEM((GROUP, rows, wide), F32),
                double,
                double,
                pltpu.VMEM((GROUP, width, rows), F32),
                pltpu.VMEM((GROUP, wide, rows), BF16),
                pltpu.VMEM((GROUP, wide, rows), BF16),
                pltpu.VMEM((GROUP, 2 * rows, wide), BF16),
                pltpu.VMEM((GROUP, width, rows), BF16),
            ]
            + lists(most),
            10 * unit_cost * 1280,
            10 * unit_cost,
        )(near, x, d, lse, delta, dq)[0]

    part = MINE * width // samples
    w_part = exchange(w_term.reshape(samples, part, model), "sample")
    w_part = jnp.sum(w_part.astype(F32), axis=0).astype(BF16)
    own0 = own_terms(0, lse, delta, dq)
    w_part, lse, own0 = lax.optimization_barrier((w_part, lse, own0))
    own1 = own_terms(1, lse, delta, dq)
    if alone:
        w_part = w_part.astype(F32) + across(w_part).astype(F32)
    else:
        alike = [[g * GROUP + r for g in range(groups)] for r in range(GROUP)]
        w_part = lax.psum(w_part.astype(F32), "seg", axis_index_groups=alike)
    w_part, back, own1 = lax.optimization_barrier((w_part, back, own1))
    (merged,) = call(
        functools.partial(merge_kernel, alone),
        "merge",
        [((GROUP, MINE * (rows + 2 * half), wide), BF16)],
        [],
        0,
    )(own0, own1, back, attn)
    w_part, merged = lax.optimization_barrier((w_part, merged))
    home = swap(merged)
    grad_scale = 1.0 / math.sqrt(samples * rows * seg)
    w_rows = gathered((w_part * grad_scale).astype(BF16), "seg", GROUP)
    w_all = gathered(w_rows, "sample", samples)
    grad_w_out = jnp.transpose(w_all, (1, 0, 2, 3)).reshape(model, model).astype(F32)
    attended, grad_q, grad_k, grad_v = call(
        unpack_kernel, "unpack", [((rows, model), BF16)] * 4, [], 2 * rows * model * model
    )(home, w_out)
    return attended[None], grad_q[None], grad_k[None], grad_v[None], grad_w_out


def solution(mesh):
    rows = P("sample", "seg", None)
    return jax.shard_map(
        body,
        mesh=mesh,
        in_specs=(rows, rows, rows, P(), rows, rows),
        out_specs=(rows, rows, rows, rows, P()),
        check_vma=False,
    )
```

```python
import functools
import math

import jax
import jax.numpy as jnp
from jax import lax
from jax.experimental import pallas as pl
from jax.experimental.pallas import tpu as pltpu
from jax.sharding import PartitionSpec as P

HEADS = 8
NBR = 3
REACH = 3
GROUP = 4
MINE = HEADS // GROUP
F32 = jnp.float32
BF16 = jnp.bfloat16


def mm(a, b):
    return lax.dot_general(a, b, (((1,), (0,)), ((), ())), preferred_element_type=F32)


def halves(block):
    turned = block.T
    width = turned.shape[0] // 2
    return jnp.concatenate([turned[:width], turned[width:]], axis=1)


def beside(turned):
    rows = turned.shape[1]
    return jnp.concatenate([turned[:, : rows // 2], turned[:, rows // 2 :]], axis=0).T


def pack_kernel(near_ref, *refs):
    sources, (out_ref, spread_ref, *direct), held, arrived = refs[:5], refs[5:-6], refs[-6:-1], refs[-1]
    copies = [
        pltpu.make_async_copy(source, target, arrived.at[i])
        for i, (source, target) in enumerate(zip(sources, held))
    ]
    for copy in copies:
        copy.start()
    for copy in copies:
        copy.wait()
    q_ref, k_ref, v_ref, g_ref, w_ref = held
    rows = q_ref.shape[0]
    width = q_ref.shape[1] // HEADS
    half = rows // 2
    here = lax.axis_index("seg")
    line = lax.broadcasted_iota(jnp.int32, (16, 2 * width), 0)
    offsets = jnp.zeros((16, 2 * width), F32)
    for e in range(NBR):
        offsets = jnp.where(line == e, (near_ref[0, e] - here + REACH).astype(F32), offsets)
    d_attn = lax.dot_general(
        g_ref[...], w_ref[...], (((1,), (1,)), ((), ())), preferred_element_type=F32
    ).astype(BF16)
    for h in range(HEADS):
        to, i = divmod(h, MINE)
        cols = slice(h * width, (h + 1) * width)
        at_q = MINE * rows + i * half
        at_d = MINE * (rows + half) + i * half
        out_ref[to, i * rows : (i + 1) * rows, :] = jnp.concatenate(
            [k_ref[:, cols], v_ref[:, cols]], axis=1
        )
        out_ref[to, at_q : at_q + half, :] = jnp.concatenate(
            [q_ref[:half, cols], q_ref[half:, cols]], axis=1
        )
        out_ref[to, at_d : at_d + half, :] = jnp.concatenate(
            [d_attn[:half, cols], d_attn[half:, cols]], axis=1
        )
        out_ref[to, MINE * (rows + 2 * half) :, :] = offsets.astype(BF16)
    for to in range(GROUP):
        spread_ref[to] = g_ref[...]
    for by, ref in enumerate(direct):
        ref[...] = out_ref[(here % GROUP) ^ by, : MINE * rows, :]


def list_units(near_ref, patch_of, block_of, count, first, outside, right=0, base=0):
    for p in range(GROUP):
        if not outside:
            patch_of[count] = first + p
            block_of[count] = base + p
            count = count + 1
        for e in range(NBR):
            t = p + near_ref[p, e] - REACH
            inside = jnp.logical_and(t >= 0, t < GROUP)
            patch_of[count] = first + p
            if outside:
                want = jnp.logical_not(inside)
                block_of[count] = base + jnp.where(t < 0, t + REACH, t - GROUP + right)
            else:
                want = jnp.logical_and(inside, t != p)
                block_of[count] = base + t
            count = count + jnp.where(want, 1, 0)
    return count


def in_turn(total, enter, leave):
    def both(u, slot):
        leave(u, slot, lambda: enter(u + 1, 1 - slot))

    def two(i, carry):
        both(2 * i, 0)
        both(2 * i + 1, 1)
        return carry

    @pl.when(total > 0)
    def _():
        enter(jnp.int32(0), 0)
        lax.fori_loop(0, (total - 1) // 2, two, 0)
        pl.when(total % 2 == 0)(lambda: both(total - 2, 0))
        for slot in range(2):

            @pl.when((total - 1) % 2 == slot)
            def _():
                leave(total - 1, slot, lambda: None)


def mix_units(total, patch_of, block_of, keys, q_scr, v_scr, scores, before_scr, top_scr, m_ref, o_ref):
    def enter(u, slot):
        p = patch_of[u]
        s = mm(keys(block_of[u]), q_scr[p])
        scores[slot][...] = s
        before = m_ref[p]
        top = jnp.maximum(before, jnp.max(s, axis=0, keepdims=True))
        before_scr[u] = before
        top_scr[u] = top
        m_ref[p] = top

    def leave(u, slot, then):
        p, top = patch_of[u], top_scr[u]
        prob = jnp.exp(scores[slot][...] - top).astype(BF16)
        keep = jnp.exp(before_scr[u] - top)
        then()
        o_ref[p] = o_ref[p] * keep + mm(v_scr[block_of[u]], prob)

    in_turn(total, enter, leave)


def back_units(total, patch_of, block_of, keys, q_scr, d_scr, back_scr, k_scr, pairs, lse_ref, delta_ref, dq_ref, acc):
    rows = q_scr.shape[2]

    def enter(u, slot):
        block, p = keys(block_of[u]), patch_of[u]
        pairs[slot][:, :rows] = mm(block, q_scr[p])
        pairs[slot][:, rows:] = mm(block, d_scr[p])

    def leave(u, slot, then):
        b, p = block_of[u], patch_of[u]
        prob = jnp.exp(pairs[slot][:, :rows] - lse_ref[p])
        ds = (prob * (pairs[slot][:, rows:] - delta_ref[p])).astype(BF16)
        then()
        dq_ref[p] += mm(k_scr[b], ds)
        acc[b] += mm(jnp.concatenate([ds, prob.astype(BF16)], axis=1), back_scr[p])

    in_turn(total, enter, leave)


def fill_q(x_ref, head, rows, width, q_scr, at):
    half = rows // 2
    start = MINE * rows + head * half
    for p in range(GROUP):
        turned = halves(x_ref[p, start : start + half, :])
        q_scr[at + p, :width, :] = turned * BF16(1.0 / math.sqrt(width))
        q_scr[at + p, width:, :] = jnp.zeros_like(turned)


def fill_back(x_ref, head, rows, width, d_scr, back_scr, at=0):
    half = rows // 2
    start = MINE * rows + head * half
    blank = jnp.zeros((half, width), BF16)
    for p in range(GROUP):
        q_pair = x_ref[p, start : start + half, :]
        d_pair = x_ref[p, start + MINE * half : start + (MINE + 1) * half, :]
        back_scr[at + p, :half, :] = jnp.concatenate([q_pair[:, :width], blank], axis=1)
        back_scr[at + p, half:rows, :] = jnp.concatenate([q_pair[:, width:], blank], axis=1)
        back_scr[at + p, rows : rows + half, :] = jnp.concatenate([blank, d_pair[:, :width]], axis=1)
        back_scr[at + p, rows + half :, :] = jnp.concatenate([blank, d_pair[:, width:]], axis=1)
        d_turned = halves(d_pair)
        d_scr[at + p, :width, :] = jnp.zeros_like(d_turned)
        d_scr[at + p, width:, :] = d_turned * BF16(1.0 / math.sqrt(width))


def attend_kernel(alone, near_ref, x_ref, *refs):
    halos, refs = refs[: GROUP if alone else 1], refs[GROUP if alone else 1 :]
    (attn_ref, lse_ref, delta_ref, dq_ref, out_ref, acc, s0, s1, before_scr, top_scr, m_scr, o_scr, q_scr, d_scr, back_scr, v_scr, k_scr, kv_scr, patch_of, block_of, far_patch, far_block) = refs
    rows, width = q_scr.shape[2], x_ref.shape[2] // 2
    half, halo = rows // 2, REACH if alone else 2 * REACH
    blocks = GROUP + halo
    right = halo - REACH
    other = 1 - lax.axis_index("seg") // GROUP if alone else 0
    for b in range(GROUP):
        kv_scr[b] = x_ref[b, : MINE * rows, :]
    for b in range(halo):
        if alone:
            by = (b + 1 - other) ^ (lax.axis_index("seg") % GROUP)
            for k in range(GROUP):

                @pl.when(by == k)
                def _():
                    kv_scr[GROUP + b] = halos[k][...]

        else:
            kv_scr[GROUP + b] = halos[0][b]
    total, far_total = jnp.int32(0), jnp.int32(0)
    for i in range(MINE):
        base = i * blocks
        total = list_units(near_ref, patch_of, block_of, total, i * GROUP, False, 0, base)
        total = list_units(near_ref, patch_of, block_of, total, i * GROUP, True, right, base + GROUP)
        far_total = list_units(
            near_ref, far_patch, far_block, far_total, i * GROUP, True, right, base + GROUP
        )
        fill_q(x_ref, i, rows, width, q_scr, i * GROUP)
        fill_back(x_ref, i, rows, width, d_scr, back_scr, i * GROUP)
        for b in range(blocks):
            turned = kv_scr[b, i * rows : (i + 1) * rows, :].T
            v_scr[base + b, :width, :] = turned[width:]
            v_scr[base + b, width:, :] = jnp.ones((v_scr.shape[1] - width, rows), BF16)
            if b >= GROUP:
                k_scr[base + b] = turned[:width]
    o_scr[...] = jnp.zeros_like(o_scr)
    m_scr[...] = jnp.full_like(m_scr, -jnp.inf)

    def keys(b):
        return kv_scr[b % blocks, pl.ds(pl.multiple_of(b // blocks * rows, rows), rows), :]

    firsts = (s0.at[:, :rows], s1.at[:, :rows])
    mix_units(total, patch_of, block_of, keys, q_scr, v_scr, firsts, before_scr, top_scr, m_scr, o_scr)
    for p in range(MINE * GROUP):
        sums = o_scr[p, width : width + 1, :]
        attn = (o_scr[p, :width, :] * (1.0 / sums)).astype(BF16)
        attn_ref[p % GROUP, p // GROUP * half : (p // GROUP + 1) * half, :] = beside(attn)
        lse_ref[p] = m_scr[p] + jnp.log(sums)
        product = d_scr[p, width:, :].astype(F32) * attn.astype(F32)
        delta_ref[p] = jnp.sum(product, axis=0, keepdims=True)
    for i in range(MINE):
        for b in range(halo):
            acc[i * blocks + GROUP + b] = jnp.zeros(acc.shape[1:], F32)
    dq_ref[...] = jnp.zeros_like(dq_ref)
    back_units(far_total, far_patch, far_block, keys, q_scr, d_scr, back_scr, k_scr, (s0, s1), lse_ref, delta_ref, dq_ref, acc)
    for i in range(MINE):
        for b in range(halo):
            out_ref[b, i * rows : (i + 1) * rows, :] = acc[i * blocks + GROUP + b].astype(BF16)


def term_kernel(attn_ref, g_ref, term_ref):
    half = attn_ref.shape[1] // MINE
    term = jnp.zeros(term_ref.shape, F32)
    for p in range(GROUP):
        turned = [halves(attn_ref[p, i * half : (i + 1) * half, :]) for i in range(MINE)]
        term = term + mm(jnp.concatenate(turned, axis=0), g_ref[p])
    term_ref[...] = term.astype(BF16)


def own_kernel(head, near_ref, x_ref, lse_ref, delta_ref, dq_in, out_ref, acc, s0, s1, dq_scr, q_scr, d_scr, back_scr, k_scr, patch_of, block_of):
    rows, width = q_scr.shape[2], x_ref.shape[2] // 2
    total = list_units(near_ref, patch_of, block_of, jnp.int32(0), 0, False)
    fill_q(x_ref, head, rows, width, q_scr, 0)
    fill_back(x_ref, head, rows, width, d_scr, back_scr)
    mine = slice(head * rows, (head + 1) * rows)
    for b in range(GROUP):
        k_scr[b] = x_ref[b, mine, :].T[:width]
    own = pl.ds(head * GROUP, GROUP)
    acc[...] = jnp.zeros_like(acc)
    dq_scr[...] = dq_in[head * GROUP : (head + 1) * GROUP]
    keys = lambda b: x_ref[b, mine, :]
    back_units(total, patch_of, block_of, keys, q_scr, d_scr, back_scr, k_scr, (s0, s1), lse_ref.at[own], delta_ref.at[own], dq_scr, acc)
    for p in range(GROUP):
        out_ref[p, :rows, :] = acc[p].astype(BF16)
        out_ref[p, rows:, :] = beside(dq_scr[p].astype(BF16))


def merge_kernel(alone, *refs):
    owns, back_ref, attn_ref, out_ref = refs[:MINE], refs[MINE], refs[-2], refs[-1]
    each = owns[0].shape[1]
    rows = each * 2 // 3
    for p in range(GROUP):
        out_ref[p, MINE * each :, :] = attn_ref[p]
    for i in range(MINE):
        for p in range(GROUP):
            out_ref[p, i * each : (i + 1) * each, :] = owns[i][p]
        mine = slice(i * each, i * each + rows)
        other = 1 - lax.axis_index("seg") // GROUP if alone else 0
        for side in range(back_ref.shape[0] // REACH):
            start = other if alone else 1 - side
            for j in range(REACH):
                term = back_ref[side * REACH + j, i * rows : (i + 1) * rows, :].astype(F32)
                here = out_ref[start + j, mine, :].astype(F32)
                out_ref[start + j, mine, :] = (here + term).astype(BF16)


def unpack_kernel(y_ref, w_ref, out_ref, dq_ref, dk_ref, dv_ref):
    rows, width = dk_ref.shape[0], y_ref.shape[2] // 2
    half = rows // 2
    sides = ([], [])
    for h in range(HEADS):
        cols = slice(h * width, (h + 1) * width)
        r, i = divmod(h, MINE)
        at = i * (rows + half)
        dk_ref[:, cols] = y_ref[r, at : at + rows, :width]
        dv_ref[:, cols] = y_ref[r, at : at + rows, width:]
        dq_ref[:half, cols] = y_ref[r, at + rows : at + rows + half, :width]
        dq_ref[half:, cols] = y_ref[r, at + rows : at + rows + half, width:]
        at = MINE * (rows + half) + i * half
        sides[0].append(y_ref[r, at : at + half, :width])
        sides[1].append(y_ref[r, at : at + half, width:])
    attn = jnp.concatenate([jnp.concatenate(side, axis=1) for side in sides], axis=0)
    out_ref[...] = mm(attn, w_ref[...]).astype(BF16)


def params(mib=32):
    return pltpu.CompilerParams(vmem_limit_bytes=mib * 2**20)


def cost(flops, bytes_accessed, exps=0):
    return pl.CostEstimate(flops=flops // 1000, bytes_accessed=bytes_accessed // 1000, transcendentals=0)


def in_hbm(array):
    return pltpu.with_memory_space_constraint(array, pltpu.HBM)


def around(count, by):
    return [(i, (i + by) % count) for i in range(count)]


def exchange(pieces, axis):
    count = pieces.shape[0]
    if count > HEADS:
        return lax.all_to_all(pieces, axis, 0, 0)
    here = lax.axis_index(axis)
    arrived = []
    for by in range(count):
        piece = lax.dynamic_index_in_dim(pieces, (here + by) % count, 0, keepdims=False)
        arrived.append(lax.ppermute(piece, axis, around(count, by)) if by else piece)
    return jnp.stack(arrived)


def gathered(piece, axis, count):
    size = lax.axis_size(axis)
    here = lax.axis_index(axis) % count
    arrived = [piece]
    for by in range(1, count):
        pairs = [(i, i // count * count + (i + by) % count) for i in range(size)]
        arrived.append(lax.ppermute(piece, axis, pairs))
    line = jnp.stack(arrived[::-1] + arrived[::-1])
    return lax.dynamic_slice_in_dim(line, count - 1 - here, count, 0)


def body(queries, key_rows, value_rows, w_out, grad_out, neighbours):
    _, rows, model = queries.shape
    width = model // HEADS
    half, wide = rows // 2, 2 * width
    seg = lax.axis_size("seg")
    samples = lax.axis_size("sample")
    groups = seg // GROUP
    split = [[g * GROUP + i for i in range(GROUP)] for g in range(groups)]
    alone = groups == 2
    halo = REACH if alone else 2 * REACH
    ones = 16
    most = GROUP * (NBR + 1)
    vmem = pl.BlockSpec(memory_space=pltpu.VMEM)
    smem = pl.BlockSpec(memory_space=pltpu.SMEM)
    unit_cost = rows * rows

    def swap(array):
        return lax.all_to_all(array, "seg", 0, 0, axis_index_groups=split)

    def shifted(array, by):
        pairs = [(s, s + by) for s in range(seg) if 0 <= s + by < seg]
        return lax.ppermute(array, "seg", pairs)

    def across(array):
        return lax.ppermute(array, "seg", [(s, (s + GROUP) % seg) for s in range(seg)])

    def between(array):
        pairs = [[i, i + GROUP] for i in range(GROUP)]
        return lax.all_to_all(array, "seg", 0, 0, axis_index_groups=pairs)

    def call(kernel, name, outs, scratch, flops, exps=0, mib=32):
        return pl.pallas_call(
            kernel,
            out_shape=[jax.ShapeDtypeStruct(shape, kind) for shape, kind in outs],
            out_specs=[vmem] * len(outs),
            scratch_shapes=scratch,
            compiler_params=params(mib),
            cost_estimate=cost(flops, 4 * 2**20, exps),
            name=name,
        )

    packed, spread, *direct = pl.pallas_call(
        pack_kernel,
        in_specs=[smem] + [pl.BlockSpec(memory_space=pltpu.HBM)] * 5,
        scratch_shapes=[pltpu.VMEM((rows, model), BF16)] * 4
        + [pltpu.VMEM((model, model), BF16), pltpu.SemaphoreType.DMA((5,))],
        out_shape=[
            jax.ShapeDtypeStruct((GROUP, MINE * (rows + 2 * half) + 16, wide), BF16),
            jax.ShapeDtypeStruct((GROUP, rows, model), BF16),
        ]
        + [jax.ShapeDtypeStruct((MINE * rows, wide), BF16)] * (GROUP if alone else 0),
        compiler_params=params(60),
        cost_estimate=cost(2 * rows * model * model, 10 * rows * model),
        name="pack",
    )(
        neighbours[0],
        *(in_hbm(a) for a in (queries[0], key_rows[0], value_rows[0], grad_out[0], w_out)),
    )
    x = swap(packed)
    if alone:
        border = [g * GROUP + i for g in range(2) for i in range(1 - g, 1 - g + REACH)]
        beyond = [
            lax.ppermute(array, "seg", [(s, (s + GROUP) % seg ^ by) for s in border])
            for by, array in enumerate(direct)
        ]
    else:
        kv = x[:, : MINE * rows]
        beyond = [
            jnp.concatenate([shifted(kv[1:], GROUP), shifted(kv[:REACH], -GROUP)], axis=0)
        ]
    at = MINE * (rows + 2 * half)
    near = x[:, at : at + NBR, 0].astype(jnp.int32)
    x, near, beyond, spread = lax.optimization_barrier((x, near, beyond, spread))
    grads_here = swap(spread)

    lists = lambda count: [pltpu.SMEM((count + 8,), jnp.int32)] * 2
    sheet = pltpu.VMEM((rows, rows), F32)
    double = pltpu.VMEM((rows, 2 * rows), F32)
    lines = lambda count: pltpu.VMEM((count, 1, rows), F32)
    patches = MINE * GROUP
    blocks = GROUP + halo
    attn, lse, delta, dq, far = call(
        functools.partial(attend_kernel, alone),
        "attend",
        [
            ((GROUP, MINE * half, wide), BF16),
            ((patches, 1, rows), F32),
            ((patches, 1, rows), F32),
            ((patches, width, rows), F32),
            ((halo, MINE * rows, wide), BF16),
        ],
        [
            pltpu.VMEM((MINE * blocks, rows, wide), F32),
            double,
            double,
            lines(MINE * most),
            lines(MINE * most),
            lines(patches),
            pltpu.VMEM((patches, width + ones, rows), F32),
            pltpu.VMEM((patches, wide, rows), BF16),
            pltpu.VMEM((patches, wide, rows), BF16),
            pltpu.VMEM((patches, 2 * rows, wide), BF16),
            pltpu.VMEM((MINE * blocks, width + ones, rows), BF16),
            pltpu.VMEM((MINE * blocks, width, rows), BF16),
            pltpu.VMEM((blocks, MINE * rows, wide), BF16),
        ]
        + lists(MINE * most)
        + lists(MINE * most),
        6 * unit_cost * 1536,
        12 * unit_cost,
        60,
    )(near, x, *beyond)
    if alone:
        back = across(far)
    else:
        back = jnp.concatenate([shifted(far[:REACH], -GROUP), shifted(far[REACH:], GROUP)], axis=0)

    def own_terms(i, lse, delta, dq):
        return call(
            functools.partial(own_kernel, i),
            f"own{i}",
            [((GROUP, rows + half, wide), BF16)],
            [
                pltpu.VMEM((GROUP, rows, wide), F32),
                double,
                double,
                pltpu.VMEM((GROUP, width, rows), F32),
                pltpu.VMEM((GROUP, wide, rows), BF16),
                pltpu.VMEM((GROUP, wide, rows), BF16),
                pltpu.VMEM((GROUP, 2 * rows, wide), BF16),
                pltpu.VMEM((GROUP, width, rows), BF16),
            ]
            + lists(most),
            10 * unit_cost * 1280,
            10 * unit_cost,
        )(near, x, lse, delta, dq)[0]

    part = MINE * width // samples
    (w_term,) = call(
        term_kernel, "term", [((MINE * width, model), BF16)], [], 2 * rows * model * model
    )(attn, grads_here)
    w_part = exchange(w_term.reshape(samples, part, model), "sample")
    w_part = jnp.sum(w_part.astype(F32), axis=0).astype(BF16)
    own0 = own_terms(0, lse, delta, dq)
    w_part, lse, own0 = lax.optimization_barrier((w_part, lse, own0))
    own1 = own_terms(1, lse, delta, dq)
    if alone:
        w_part = w_part.astype(F32) + across(w_part).astype(F32)
    else:
        alike = [[g * GROUP + r for g in range(groups)] for r in range(GROUP)]
        w_part = lax.psum(w_part.astype(F32), "seg", axis_index_groups=alike)
    w_part, back, own1 = lax.optimization_barrier((w_part, back, own1))
    (merged,) = call(
        functools.partial(merge_kernel, alone),
        "merge",
        [((GROUP, MINE * (rows + 2 * half), wide), BF16)],
        [],
        0,
    )(own0, own1, back, attn)
    w_part, merged = lax.optimization_barrier((w_part, merged))
    home = swap(merged)
    grad_scale = 1.0 / math.sqrt(samples * rows * seg)
    w_rows = gathered((w_part * grad_scale).astype(BF16), "seg", GROUP)
    w_all = gathered(w_rows, "sample", samples)
    grad_w_out = jnp.transpose(w_all, (1, 0, 2, 3)).reshape(model, model).astype(F32)
    attended, grad_q, grad_k, grad_v = call(
        unpack_kernel, "unpack", [((rows, model), BF16)] * 4, [], 2 * rows * model * model
    )(home, w_out)
    return attended[None], grad_q[None], grad_k[None], grad_v[None], grad_w_out


def solution(mesh):
    rows = P("sample", "seg", None)
    return jax.shard_map(
        body,
        mesh=mesh,
        in_specs=(rows, rows, rows, P(), rows, rows),
        out_specs=(rows, rows, rows, rows, P()),
        check_vma=False,
    )
```

```python
import functools
import math

import jax
import jax.numpy as jnp
from jax import lax
from jax.experimental import pallas as pl
from jax.experimental.pallas import tpu as pltpu
from jax.sharding import PartitionSpec as P

HEADS = 8
NBR = 3
REACH = 3
GROUP = 4
MINE = HEADS // GROUP
F32 = jnp.float32
BF16 = jnp.bfloat16


def mm(a, b):
    return lax.dot_general(a, b, (((1,), (0,)), ((), ())), preferred_element_type=F32)


def halves(block):
    turned = block.T
    width = turned.shape[0] // 2
    return jnp.concatenate([turned[:width], turned[width:]], axis=1)


def beside(turned):
    rows = turned.shape[1]
    return jnp.concatenate([turned[:, : rows // 2], turned[:, rows // 2 :]], axis=0).T


def pack_kernel(near_ref, *refs):
    sources, (out_ref, *direct), held, arrived = refs[:5], refs[5:-6], refs[-6:-1], refs[-1]
    copies = [
        pltpu.make_async_copy(source, target, arrived.at[i])
        for i, (source, target) in enumerate(zip(sources, held))
    ]
    for copy in copies:
        copy.start()
    for copy in copies:
        copy.wait()
    q_ref, k_ref, v_ref, g_ref, w_ref = held
    rows = q_ref.shape[0]
    width = q_ref.shape[1] // HEADS
    half = rows // 2
    here = lax.axis_index("seg")
    line = lax.broadcasted_iota(jnp.int32, (16, 2 * width), 0)
    offsets = jnp.zeros((16, 2 * width), F32)
    for e in range(NBR):
        offsets = jnp.where(line == e, (near_ref[0, e] - here + REACH).astype(F32), offsets)
    d_attn = lax.dot_general(
        g_ref[...], w_ref[...], (((1,), (1,)), ((), ())), preferred_element_type=F32
    ).astype(BF16)
    for h in range(HEADS):
        to, i = divmod(h, MINE)
        cols = slice(h * width, (h + 1) * width)
        at_q = MINE * rows + i * half
        at_d = MINE * (rows + half) + i * half
        out_ref[to, i * rows : (i + 1) * rows, :] = jnp.concatenate(
            [k_ref[:, cols], v_ref[:, cols]], axis=1
        )
        out_ref[to, at_q : at_q + half, :] = jnp.concatenate(
            [q_ref[:half, cols], q_ref[half:, cols]], axis=1
        )
        out_ref[to, at_d : at_d + half, :] = jnp.concatenate(
            [d_attn[:half, cols], d_attn[half:, cols]], axis=1
        )
        out_ref[to, MINE * (rows + 2 * half) :, :] = offsets.astype(BF16)
    for by, ref in enumerate(direct):
        ref[...] = out_ref[(here % GROUP) ^ by, : MINE * rows, :]


def list_units(near_ref, patch_of, block_of, count, first, outside, right=0, base=0):
    for p in range(GROUP):
        if not outside:
            patch_of[count] = first + p
            block_of[count] = base + p
            count = count + 1
        for e in range(NBR):
            t = p + near_ref[p, e] - REACH
            inside = jnp.logical_and(t >= 0, t < GROUP)
            patch_of[count] = first + p
            if outside:
                want = jnp.logical_not(inside)
                block_of[count] = base + jnp.where(t < 0, t + REACH, t - GROUP + right)
            else:
                want = jnp.logical_and(inside, t != p)
                block_of[count] = base + t
            count = count + jnp.where(want, 1, 0)
    return count


def in_turn(total, enter, leave):
    def both(u, slot):
        leave(u, slot, lambda: enter(u + 1, 1 - slot))

    def two(i, carry):
        both(2 * i, 0)
        both(2 * i + 1, 1)
        return carry

    @pl.when(total > 0)
    def _():
        enter(jnp.int32(0), 0)
        lax.fori_loop(0, (total - 1) // 2, two, 0)
        pl.when(total % 2 == 0)(lambda: both(total - 2, 0))
        for slot in range(2):

            @pl.when((total - 1) % 2 == slot)
            def _():
                leave(total - 1, slot, lambda: None)


def mix_units(total, patch_of, block_of, keys, q_scr, v_scr, scores, before_scr, top_scr, m_ref, o_ref):
    def enter(u, slot):
        p = patch_of[u]
        s = mm(keys(block_of[u]), q_scr[p])
        scores[slot][...] = s
        before = m_ref[p]
        top = jnp.maximum(before, jnp.max(s, axis=0, keepdims=True))
        before_scr[u] = before
        top_scr[u] = top
        m_ref[p] = top

    def leave(u, slot, then):
        p, top = patch_of[u], top_scr[u]
        prob = jnp.exp(scores[slot][...] - top).astype(BF16)
        keep = jnp.exp(before_scr[u] - top)
        then()
        o_ref[p] = o_ref[p] * keep + mm(v_scr[block_of[u]], prob)

    in_turn(total, enter, leave)


def back_units(total, patch_of, block_of, keys, q_scr, d_scr, back_scr, k_scr, pairs, lse_ref, delta_ref, dq_ref, acc):
    rows = q_scr.shape[2]

    def enter(u, slot):
        block, p = keys(block_of[u]), patch_of[u]
        pairs[slot][:, :rows] = mm(block, q_scr[p])
        pairs[slot][:, rows:] = mm(block, d_scr[p])

    def leave(u, slot, then):
        b, p = block_of[u], patch_of[u]
        prob = jnp.exp(pairs[slot][:, :rows] - lse_ref[p])
        ds = (prob * (pairs[slot][:, rows:] - delta_ref[p])).astype(BF16)
        then()
        dq_ref[p] += mm(k_scr[b], ds)
        acc[b] += mm(jnp.concatenate([ds, prob.astype(BF16)], axis=1), back_scr[p])

    in_turn(total, enter, leave)


def fill_q(x_ref, head, rows, width, q_scr, at):
    half = rows // 2
    start = MINE * rows + head * half
    for p in range(GROUP):
        turned = halves(x_ref[p, start : start + half, :])
        q_scr[at + p, :width, :] = turned * BF16(1.0 / math.sqrt(width))
        q_scr[at + p, width:, :] = jnp.zeros_like(turned)


def fill_back(x_ref, head, rows, width, d_scr, back_scr, at=0):
    half = rows // 2
    start = MINE * rows + head * half
    blank = jnp.zeros((half, width), BF16)
    for p in range(GROUP):
        q_pair = x_ref[p, start : start + half, :]
        d_pair = x_ref[p, start + MINE * half : start + (MINE + 1) * half, :]
        back_scr[at + p, :half, :] = jnp.concatenate([q_pair[:, :width], blank], axis=1)
        back_scr[at + p, half:rows, :] = jnp.concatenate([q_pair[:, width:], blank], axis=1)
        back_scr[at + p, rows : rows + half, :] = jnp.concatenate([blank, d_pair[:, :width]], axis=1)
        back_scr[at + p, rows + half :, :] = jnp.concatenate([blank, d_pair[:, width:]], axis=1)
        d_turned = halves(d_pair)
        d_scr[at + p, :width, :] = jnp.zeros_like(d_turned)
        d_scr[at + p, width:, :] = d_turned * BF16(1.0 / math.sqrt(width))


def attend_kernel(alone, near_ref, x_ref, *refs):
    halos, refs = refs[: GROUP if alone else 1], refs[GROUP if alone else 1 :]
    (attn_ref, lse_ref, delta_ref, dq_ref, out_ref, acc, s0, s1, before_scr, top_scr, m_scr, o_scr, q_scr, d_scr, back_scr, v_scr, k_scr, kv_scr, patch_of, block_of, far_patch, far_block) = refs
    rows, width = q_scr.shape[2], x_ref.shape[2] // 2
    half, halo = rows // 2, REACH if alone else 2 * REACH
    blocks = GROUP + halo
    right = halo - REACH
    other = 1 - lax.axis_index("seg") // GROUP if alone else 0
    for b in range(GROUP):
        kv_scr[b] = x_ref[b, : MINE * rows, :]
    for b in range(halo):
        if alone:
            by = (b + 1 - other) ^ (lax.axis_index("seg") % GROUP)
            for k in range(GROUP):

                @pl.when(by == k)
                def _():
                    kv_scr[GROUP + b] = halos[k][...]

        else:
            kv_scr[GROUP + b] = halos[0][b]
    total, far_total = jnp.int32(0), jnp.int32(0)
    for i in range(MINE):
        base = i * blocks
        total = list_units(near_ref, patch_of, block_of, total, i * GROUP, False, 0, base)
        total = list_units(near_ref, patch_of, block_of, total, i * GROUP, True, right, base + GROUP)
        far_total = list_units(
            near_ref, far_patch, far_block, far_total, i * GROUP, True, right, base + GROUP
        )
        fill_q(x_ref, i, rows, width, q_scr, i * GROUP)
        fill_back(x_ref, i, rows, width, d_scr, back_scr, i * GROUP)
        for b in range(blocks):
            turned = kv_scr[b, i * rows : (i + 1) * rows, :].T
            v_scr[base + b, :width, :] = turned[width:]
            v_scr[base + b, width:, :] = jnp.ones((v_scr.shape[1] - width, rows), BF16)
            if b >= GROUP:
                k_scr[base + b] = turned[:width]
    o_scr[...] = jnp.zeros_like(o_scr)
    m_scr[...] = jnp.full_like(m_scr, -jnp.inf)

    def keys(b):
        return kv_scr[b % blocks, pl.ds(pl.multiple_of(b // blocks * rows, rows), rows), :]

    firsts = (s0.at[:, :rows], s1.at[:, :rows])
    mix_units(total, patch_of, block_of, keys, q_scr, v_scr, firsts, before_scr, top_scr, m_scr, o_scr)
    for p in range(MINE * GROUP):
        sums = o_scr[p, width : width + 1, :]
        attn = (o_scr[p, :width, :] * (1.0 / sums)).astype(BF16)
        attn_ref[p % GROUP, p // GROUP * half : (p // GROUP + 1) * half, :] = beside(attn)
        lse_ref[p] = m_scr[p] + jnp.log(sums)
        product = d_scr[p, width:, :].astype(F32) * attn.astype(F32)
        delta_ref[p] = jnp.sum(product, axis=0, keepdims=True)
    for i in range(MINE):
        for b in range(halo):
            acc[i * blocks + GROUP + b] = jnp.zeros(acc.shape[1:], F32)
    dq_ref[...] = jnp.zeros_like(dq_ref)
    back_units(far_total, far_patch, far_block, keys, q_scr, d_scr, back_scr, k_scr, (s0, s1), lse_ref, delta_ref, dq_ref, acc)
    for i in range(MINE):
        for b in range(halo):
            out_ref[b, i * rows : (i + 1) * rows, :] = acc[i * blocks + GROUP + b].astype(BF16)


def term_kernel(attn_ref, *refs):
    grads, term_ref = refs[:GROUP], refs[GROUP]
    half = attn_ref.shape[1] // MINE
    term = jnp.zeros(term_ref.shape, F32)
    for by in range(GROUP):
        p = (lax.axis_index("seg") % GROUP) ^ by
        turned = [halves(attn_ref[p, i * half : (i + 1) * half, :]) for i in range(MINE)]
        term = term + mm(jnp.concatenate(turned, axis=0), grads[by][...])
    term_ref[...] = term.astype(BF16)


def own_kernel(head, near_ref, x_ref, lse_ref, delta_ref, dq_in, out_ref, acc, s0, s1, dq_scr, q_scr, d_scr, back_scr, k_scr, patch_of, block_of):
    rows, width = q_scr.shape[2], x_ref.shape[2] // 2
    total = list_units(near_ref, patch_of, block_of, jnp.int32(0), 0, False)
    fill_q(x_ref, head, rows, width, q_scr, 0)
    fill_back(x_ref, head, rows, width, d_scr, back_scr)
    mine = slice(head * rows, (head + 1) * rows)
    for b in range(GROUP):
        k_scr[b] = x_ref[b, mine, :].T[:width]
    own = pl.ds(head * GROUP, GROUP)
    acc[...] = jnp.zeros_like(acc)
    dq_scr[...] = dq_in[head * GROUP : (head + 1) * GROUP]
    keys = lambda b: x_ref[b, mine, :]
    back_units(total, patch_of, block_of, keys, q_scr, d_scr, back_scr, k_scr, (s0, s1), lse_ref.at[own], delta_ref.at[own], dq_scr, acc)
    for p in range(GROUP):
        out_ref[p, :rows, :] = acc[p].astype(BF16)
        out_ref[p, rows:, :] = beside(dq_scr[p].astype(BF16))


def merge_kernel(alone, *refs):
    owns, back_ref, attn_ref, out_ref = refs[:MINE], refs[MINE], refs[-2], refs[-1]
    each = owns[0].shape[1]
    rows = each * 2 // 3
    for p in range(GROUP):
        out_ref[p, MINE * each :, :] = attn_ref[p]
    for i in range(MINE):
        for p in range(GROUP):
            out_ref[p, i * each : (i + 1) * each, :] = owns[i][p]
        mine = slice(i * each, i * each + rows)
        other = 1 - lax.axis_index("seg") // GROUP if alone else 0
        for side in range(back_ref.shape[0] // REACH):
            start = other if alone else 1 - side
            for j in range(REACH):
                term = back_ref[side * REACH + j, i * rows : (i + 1) * rows, :].astype(F32)
                here = out_ref[start + j, mine, :].astype(F32)
                out_ref[start + j, mine, :] = (here + term).astype(BF16)


def unpack_kernel(y_ref, w_ref, out_ref, dq_ref, dk_ref, dv_ref):
    rows, width = dk_ref.shape[0], y_ref.shape[2] // 2
    half = rows // 2
    sides = ([], [])
    for h in range(HEADS):
        cols = slice(h * width, (h + 1) * width)
        r, i = divmod(h, MINE)
        at = i * (rows + half)
        dk_ref[:, cols] = y_ref[r, at : at + rows, :width]
        dv_ref[:, cols] = y_ref[r, at : at + rows, width:]
        dq_ref[:half, cols] = y_ref[r, at + rows : at + rows + half, :width]
        dq_ref[half:, cols] = y_ref[r, at + rows : at + rows + half, width:]
        at = MINE * (rows + half) + i * half
        sides[0].append(y_ref[r, at : at + half, :width])
        sides[1].append(y_ref[r, at : at + half, width:])
    attn = jnp.concatenate([jnp.concatenate(side, axis=1) for side in sides], axis=0)
    out_ref[...] = mm(attn, w_ref[...]).astype(BF16)


def params(mib=32):
    return pltpu.CompilerParams(vmem_limit_bytes=mib * 2**20)


def cost(flops, bytes_accessed, exps=0):
    return pl.CostEstimate(flops=flops // 1000, bytes_accessed=bytes_accessed // 1000, transcendentals=0)


def in_hbm(array):
    return pltpu.with_memory_space_constraint(array, pltpu.HBM)


def around(count, by):
    return [(i, (i + by) % count) for i in range(count)]


def exchange(pieces, axis):
    count = pieces.shape[0]
    if count > HEADS:
        return lax.all_to_all(pieces, axis, 0, 0)
    here = lax.axis_index(axis)
    arrived = []
    for by in range(count):
        piece = lax.dynamic_index_in_dim(pieces, (here + by) % count, 0, keepdims=False)
        arrived.append(lax.ppermute(piece, axis, around(count, by)) if by else piece)
    return jnp.stack(arrived)


def gathered(piece, axis, count):
    size = lax.axis_size(axis)
    here = lax.axis_index(axis) % count
    arrived = [piece]
    for by in range(1, count):
        pairs = [(i, i // count * count + (i + by) % count) for i in range(size)]
        arrived.append(lax.ppermute(piece, axis, pairs))
    line = jnp.stack(arrived[::-1] + arrived[::-1])
    return lax.dynamic_slice_in_dim(line, count - 1 - here, count, 0)


def body(queries, key_rows, value_rows, w_out, grad_out, neighbours):
    _, rows, model = queries.shape
    width = model // HEADS
    half, wide = rows // 2, 2 * width
    seg = lax.axis_size("seg")
    samples = lax.axis_size("sample")
    groups = seg // GROUP
    split = [[g * GROUP + i for i in range(GROUP)] for g in range(groups)]
    alone = groups == 2
    halo = REACH if alone else 2 * REACH
    ones = 16
    most = GROUP * (NBR + 1)
    vmem = pl.BlockSpec(memory_space=pltpu.VMEM)
    smem = pl.BlockSpec(memory_space=pltpu.SMEM)
    unit_cost = rows * rows

    def swap(array):
        return lax.all_to_all(array, "seg", 0, 0, axis_index_groups=split)

    def shifted(array, by):
        pairs = [(s, s + by) for s in range(seg) if 0 <= s + by < seg]
        return lax.ppermute(array, "seg", pairs)

    def across(array):
        return lax.ppermute(array, "seg", [(s, (s + GROUP) % seg) for s in range(seg)])

    def between(array):
        pairs = [[i, i + GROUP] for i in range(GROUP)]
        return lax.all_to_all(array, "seg", 0, 0, axis_index_groups=pairs)

    def call(kernel, name, outs, scratch, flops, exps=0, mib=32):
        return pl.pallas_call(
            kernel,
            out_shape=[jax.ShapeDtypeStruct(shape, kind) for shape, kind in outs],
            out_specs=[vmem] * len(outs),
            scratch_shapes=scratch,
            compiler_params=params(mib),
            cost_estimate=cost(flops, 4 * 2**20, exps),
            name=name,
        )

    packed, *direct = pl.pallas_call(
        pack_kernel,
        in_specs=[smem] + [pl.BlockSpec(memory_space=pltpu.HBM)] * 5,
        scratch_shapes=[pltpu.VMEM((rows, model), BF16)] * 4
        + [pltpu.VMEM((model, model), BF16), pltpu.SemaphoreType.DMA((5,))],
        out_shape=[
            jax.ShapeDtypeStruct((GROUP, MINE * (rows + 2 * half) + 16, wide), BF16),
        ]
        + [jax.ShapeDtypeStruct((MINE * rows, wide), BF16)] * (GROUP if alone else 0),
        compiler_params=params(60),
        cost_estimate=cost(2 * rows * model * model, 10 * rows * model),
        name="pack",
    )(
        neighbours[0],
        *(in_hbm(a) for a in (queries[0], key_rows[0], value_rows[0], grad_out[0], w_out)),
    )
    x = swap(packed)
    if alone:
        border = [g * GROUP + i for g in range(2) for i in range(1 - g, 1 - g + REACH)]
        beyond = [
            lax.ppermute(array, "seg", [(s, (s + GROUP) % seg ^ by) for s in border])
            for by, array in enumerate(direct)
        ]
    else:
        kv = x[:, : MINE * rows]
        beyond = [
            jnp.concatenate([shifted(kv[1:], GROUP), shifted(kv[:REACH], -GROUP)], axis=0)
        ]
    at = MINE * (rows + 2 * half)
    near = x[:, at : at + NBR, 0].astype(jnp.int32)
    x, near, beyond, grad_in = lax.optimization_barrier((x, near, beyond, grad_out[0]))
    grads_here = [grad_in] + [
        lax.ppermute(grad_in, "seg", [(s, s ^ by) for s in range(seg)]) for by in range(1, GROUP)
    ]

    lists = lambda count: [pltpu.SMEM((count + 8,), jnp.int32)] * 2
    sheet = pltpu.VMEM((rows, rows), F32)
    double = pltpu.VMEM((rows, 2 * rows), F32)
    lines = lambda count: pltpu.VMEM((count, 1, rows), F32)
    patches = MINE * GROUP
    blocks = GROUP + halo
    attn, lse, delta, dq, far = call(
        functools.partial(attend_kernel, alone),
        "attend",
        [
            ((GROUP, MINE * half, wide), BF16),
            ((patches, 1, rows), F32),
            ((patches, 1, rows), F32),
            ((patches, width, rows), F32),
            ((halo, MINE * rows, wide), BF16),
        ],
        [
            pltpu.VMEM((MINE * blocks, rows, wide), F32),
            double,
            double,
            lines(MINE * most),
            lines(MINE * most),
            lines(patches),
            pltpu.VMEM((patches, width + ones, rows), F32),
            pltpu.VMEM((patches, wide, rows), BF16),
            pltpu.VMEM((patches, wide, rows), BF16),
            pltpu.VMEM((patches, 2 * rows, wide), BF16),
            pltpu.VMEM((MINE * blocks, width + ones, rows), BF16),
            pltpu.VMEM((MINE * blocks, width, rows), BF16),
            pltpu.VMEM((blocks, MINE * rows, wide), BF16),
        ]
        + lists(MINE * most)
        + lists(MINE * most),
        6 * unit_cost * 1536,
        12 * unit_cost,
        60,
    )(near, x, *beyond)
    if alone:
        back = across(far)
    else:
        back = jnp.concatenate([shifted(far[:REACH], -GROUP), shifted(far[REACH:], GROUP)], axis=0)

    def own_terms(i, lse, delta, dq):
        return call(
            functools.partial(own_kernel, i),
            f"own{i}",
            [((GROUP, rows + half, wide), BF16)],
            [
                pltpu.VMEM((GROUP, rows, wide), F32),
                double,
                double,
                pltpu.VMEM((GROUP, width, rows), F32),
                pltpu.VMEM((GROUP, wide, rows), BF16),
                pltpu.VMEM((GROUP, wide, rows), BF16),
                pltpu.VMEM((GROUP, 2 * rows, wide), BF16),
                pltpu.VMEM((GROUP, width, rows), BF16),
            ]
            + lists(most),
            10 * unit_cost * 1280,
            10 * unit_cost,
        )(near, x, lse, delta, dq)[0]

    part = MINE * width // samples
    (w_term,) = call(
        term_kernel, "term", [((MINE * width, model), BF16)], [], 2 * rows * model * model
    )(attn, *grads_here)
    w_part = exchange(w_term.reshape(samples, part, model), "sample")
    w_part = jnp.sum(w_part.astype(F32), axis=0).astype(BF16)
    own0 = own_terms(0, lse, delta, dq)
    w_part, lse, own0 = lax.optimization_barrier((w_part, lse, own0))
    own1 = own_terms(1, lse, delta, dq)
    if alone:
        w_part = w_part.astype(F32) + across(w_part).astype(F32)
    else:
        alike = [[g * GROUP + r for g in range(groups)] for r in range(GROUP)]
        w_part = lax.psum(w_part.astype(F32), "seg", axis_index_groups=alike)
    w_part, back, own1 = lax.optimization_barrier((w_part, back, own1))
    (merged,) = call(
        functools.partial(merge_kernel, alone),
        "merge",
        [((GROUP, MINE * (rows + 2 * half), wide), BF16)],
        [],
        0,
    )(own0, own1, back, attn)
    w_part, merged = lax.optimization_barrier((w_part, merged))
    home = swap(merged)
    grad_scale = 1.0 / math.sqrt(samples * rows * seg)
    w_rows = gathered((w_part * grad_scale).astype(BF16), "seg", GROUP)
    w_all = gathered(w_rows, "sample", samples)
    grad_w_out = jnp.transpose(w_all, (1, 0, 2, 3)).reshape(model, model).astype(F32)
    attended, grad_q, grad_k, grad_v = call(
        unpack_kernel, "unpack", [((rows, model), BF16)] * 4, [], 2 * rows * model * model
    )(home, w_out)
    return attended[None], grad_q[None], grad_k[None], grad_v[None], grad_w_out


def solution(mesh):
    rows = P("sample", "seg", None)
    return jax.shard_map(
        body,
        mesh=mesh,
        in_specs=(rows, rows, rows, P(), rows, rows),
        out_specs=(rows, rows, rows, rows, P()),
        check_vma=False,
    )
```

```python
import functools
import math

import jax
import jax.numpy as jnp
from jax import lax
from jax.experimental import pallas as pl
from jax.experimental.pallas import tpu as pltpu
from jax.sharding import PartitionSpec as P

HEADS = 8
NBR = 3
REACH = 3
GROUP = 4
MINE = HEADS // GROUP
F32 = jnp.float32
BF16 = jnp.bfloat16


def mm(a, b):
    return lax.dot_general(a, b, (((1,), (0,)), ((), ())), preferred_element_type=F32)


def halves(block):
    turned = block.T
    width = turned.shape[0] // 2
    return jnp.concatenate([turned[:width], turned[width:]], axis=1)


def beside(turned):
    rows = turned.shape[1]
    return jnp.concatenate([turned[:, : rows // 2], turned[:, rows // 2 :]], axis=0).T


def pack_kernel(near_ref, *refs):
    sources, (out_ref, *direct), held, arrived = refs[:5], refs[5:-6], refs[-6:-1], refs[-1]
    copies = [
        pltpu.make_async_copy(source, target, arrived.at[i])
        for i, (source, target) in enumerate(zip(sources, held))
    ]
    for copy in copies:
        copy.start()
    for copy in copies:
        copy.wait()
    q_ref, k_ref, v_ref, g_ref, w_ref = held
    rows = q_ref.shape[0]
    width = q_ref.shape[1] // HEADS
    half = rows // 2
    here = lax.axis_index("seg")
    line = lax.broadcasted_iota(jnp.int32, (16, 2 * width), 0)
    offsets = jnp.zeros((16, 2 * width), F32)
    for e in range(NBR):
        offsets = jnp.where(line == e, (near_ref[0, e] - here + REACH).astype(F32), offsets)
    d_attn = lax.dot_general(
        g_ref[...], w_ref[...], (((1,), (1,)), ((), ())), preferred_element_type=F32
    ).astype(BF16)
    for h in range(HEADS):
        to, i = divmod(h, MINE)
        cols = slice(h * width, (h + 1) * width)
        at_q = MINE * rows + i * half
        at_d = MINE * (rows + half) + i * half
        out_ref[to, i * rows : (i + 1) * rows, :] = jnp.concatenate(
            [k_ref[:, cols], v_ref[:, cols]], axis=1
        )
        out_ref[to, at_q : at_q + half, :] = jnp.concatenate(
            [q_ref[:half, cols], q_ref[half:, cols]], axis=1
        )
        out_ref[to, at_d : at_d + half, :] = jnp.concatenate(
            [d_attn[:half, cols], d_attn[half:, cols]], axis=1
        )
        out_ref[to, MINE * (rows + 2 * half) :, :] = offsets.astype(BF16)
    for by, ref in enumerate(direct):
        ref[...] = out_ref[(here % GROUP) ^ by, : MINE * rows, :]


def list_units(near_ref, patch_of, block_of, count, first, outside, right=0, base=0):
    for p in range(GROUP):
        if not outside:
            patch_of[count] = first + p
            block_of[count] = base + p
            count = count + 1
        for e in range(NBR):
            t = p + near_ref[p, e] - REACH
            inside = jnp.logical_and(t >= 0, t < GROUP)
            patch_of[count] = first + p
            if outside:
                want = jnp.logical_not(inside)
                block_of[count] = base + jnp.where(t < 0, t + REACH, t - GROUP + right)
            else:
                want = jnp.logical_and(inside, t != p)
                block_of[count] = base + t
            count = count + jnp.where(want, 1, 0)
    return count


def in_turn(total, enter, leave):
    def both(u, slot):
        leave(u, slot, lambda: enter(u + 1, 1 - slot))

    def two(i, carry):
        both(2 * i, 0)
        both(2 * i + 1, 1)
        return carry

    @pl.when(total > 0)
    def _():
        enter(jnp.int32(0), 0)
        lax.fori_loop(0, (total - 1) // 2, two, 0)
        pl.when(total % 2 == 0)(lambda: both(total - 2, 0))
        for slot in range(2):

            @pl.when((total - 1) % 2 == slot)
            def _():
                leave(total - 1, slot, lambda: None)


def mix_units(total, patch_of, block_of, keys, q_scr, v_scr, scores, before_scr, top_scr, m_ref, o_ref):
    def enter(u, slot):
        p = patch_of[u]
        s = mm(keys(block_of[u]), q_scr[p])
        scores[slot][...] = s
        before = m_ref[p]
        top = jnp.maximum(before, jnp.max(s, axis=0, keepdims=True))
        before_scr[u] = before
        top_scr[u] = top
        m_ref[p] = top

    def leave(u, slot, then):
        p, top = patch_of[u], top_scr[u]
        prob = jnp.exp(scores[slot][...] - top).astype(BF16)
        keep = jnp.exp(before_scr[u] - top)
        then()
        o_ref[p] = o_ref[p] * keep + mm(v_scr[block_of[u]], prob)

    in_turn(total, enter, leave)


def back_units(total, patch_of, block_of, keys, q_scr, d_scr, back_scr, k_scr, pairs, stat_ref, dq_ref, acc):
    rows = q_scr.shape[2]

    def enter(u, slot):
        block, p = keys(block_of[u]), patch_of[u]
        pairs[slot][:, :rows] = mm(block, q_scr[p])
        pairs[slot][:, rows:] = mm(block, d_scr[p])

    def leave(u, slot, then):
        b, p = block_of[u], patch_of[u]
        prob = jnp.exp(pairs[slot][:, :rows] - stat_ref[p, :1])
        ds = (prob * (pairs[slot][:, rows:] - stat_ref[p, 1:])).astype(BF16)
        then()
        dq_ref[p] += mm(k_scr[b], ds)
        acc[b] += mm(jnp.concatenate([ds, prob.astype(BF16)], axis=1), back_scr[p])

    in_turn(total, enter, leave)


def fill_q(x_ref, head, rows, width, q_scr, at):
    half = rows // 2
    start = MINE * rows + head * half
    for p in range(GROUP):
        turned = halves(x_ref[p, start : start + half, :])
        q_scr[at + p, :width, :] = turned * BF16(1.0 / math.sqrt(width))
        q_scr[at + p, width:, :] = jnp.zeros_like(turned)


def fill_back(x_ref, head, rows, width, d_scr, back_scr, at=0):
    half = rows // 2
    start = MINE * rows + head * half
    blank = jnp.zeros((half, width), BF16)
    for p in range(GROUP):
        q_pair = x_ref[p, start : start + half, :]
        d_pair = x_ref[p, start + MINE * half : start + (MINE + 1) * half, :]
        back_scr[at + p, :half, :] = jnp.concatenate([q_pair[:, :width], blank], axis=1)
        back_scr[at + p, half:rows, :] = jnp.concatenate([q_pair[:, width:], blank], axis=1)
        back_scr[at + p, rows : rows + half, :] = jnp.concatenate([blank, d_pair[:, :width]], axis=1)
        back_scr[at + p, rows + half :, :] = jnp.concatenate([blank, d_pair[:, width:]], axis=1)
        d_turned = halves(d_pair)
        d_scr[at + p, :width, :] = jnp.zeros_like(d_turned)
        d_scr[at + p, width:, :] = d_turned * BF16(1.0 / math.sqrt(width))


def attend_kernel(alone, near_ref, x_ref, *refs):
    halos, refs = refs[: GROUP if alone else 1], refs[GROUP if alone else 1 :]
    (attn_ref, stat_ref, dq_ref, out_ref, acc, s0, s1, before_scr, top_scr, m_scr, o_scr, q_scr, d_scr, back_scr, v_scr, k_scr, kv_scr, patch_of, block_of, far_patch, far_block) = refs
    rows, width = q_scr.shape[2], x_ref.shape[2] // 2
    half, halo = rows // 2, REACH if alone else 2 * REACH
    blocks = GROUP + halo
    right = halo - REACH
    other = 1 - lax.axis_index("seg") // GROUP if alone else 0
    for b in range(GROUP):
        kv_scr[b] = x_ref[b, : MINE * rows, :]
    for b in range(halo):
        if alone:
            by = (b + 1 - other) ^ (lax.axis_index("seg") % GROUP)
            for k in range(GROUP):

                @pl.when(by == k)
                def _():
                    kv_scr[GROUP + b] = halos[k][...]

        else:
            kv_scr[GROUP + b] = halos[0][b]
    total, far_total = jnp.int32(0), jnp.int32(0)
    for i in range(MINE):
        base = i * blocks
        total = list_units(near_ref, patch_of, block_of, total, i * GROUP, False, 0, base)
        total = list_units(near_ref, patch_of, block_of, total, i * GROUP, True, right, base + GROUP)
        far_total = list_units(
            near_ref, far_patch, far_block, far_total, i * GROUP, True, right, base + GROUP
        )
        fill_q(x_ref, i, rows, width, q_scr, i * GROUP)
        fill_back(x_ref, i, rows, width, d_scr, back_scr, i * GROUP)
        for b in range(blocks):
            turned = kv_scr[b, i * rows : (i + 1) * rows, :].T
            v_scr[base + b, :width, :] = turned[width:]
            v_scr[base + b, width:, :] = jnp.ones((v_scr.shape[1] - width, rows), BF16)
            if b >= GROUP:
                k_scr[base + b] = turned[:width]
    o_scr[...] = jnp.zeros_like(o_scr)
    m_scr[...] = jnp.full_like(m_scr, -jnp.inf)

    def keys(b):
        return kv_scr[b % blocks, pl.ds(pl.multiple_of(b // blocks * rows, rows), rows), :]

    firsts = (s0.at[:, :rows], s1.at[:, :rows])
    mix_units(total, patch_of, block_of, keys, q_scr, v_scr, firsts, before_scr, top_scr, m_scr, o_scr)
    for p in range(MINE * GROUP):
        sums = o_scr[p, width : width + 1, :]
        attn = (o_scr[p, :width, :] * (1.0 / sums)).astype(BF16)
        attn_ref[p % GROUP, p // GROUP * half : (p // GROUP + 1) * half, :] = beside(attn)
        stat_ref[p, :1] = m_scr[p] + jnp.log(sums)
        product = d_scr[p, width:, :].astype(F32) * attn.astype(F32)
        stat_ref[p, 1:] = jnp.sum(product, axis=0, keepdims=True)
    for i in range(MINE):
        for b in range(halo):
            acc[i * blocks + GROUP + b] = jnp.zeros(acc.shape[1:], F32)
    dq_ref[...] = jnp.zeros_like(dq_ref)
    back_units(far_total, far_patch, far_block, keys, q_scr, d_scr, back_scr, k_scr, (s0, s1), stat_ref, dq_ref, acc)
    for i in range(MINE):
        for b in range(halo):
            out_ref[b, i * rows : (i + 1) * rows, :] = acc[i * blocks + GROUP + b].astype(BF16)


def term_kernel(attn_ref, *refs):
    grads, term_ref = refs[:GROUP], refs[GROUP]
    half = attn_ref.shape[1] // MINE
    term = jnp.zeros(term_ref.shape, F32)
    for by in range(GROUP):
        p = (lax.axis_index("seg") % GROUP) ^ by
        turned = [halves(attn_ref[p, i * half : (i + 1) * half, :]) for i in range(MINE)]
        term = term + mm(jnp.concatenate(turned, axis=0), grads[by][...])
    term_ref[...] = term.astype(BF16)


def own_kernel(head, near_ref, x_ref, stat_ref, dq_in, out_ref, acc, s0, s1, dq_scr, q_scr, d_scr, back_scr, k_scr, patch_of, block_of):
    rows, width = q_scr.shape[2], x_ref.shape[2] // 2
    total = list_units(near_ref, patch_of, block_of, jnp.int32(0), 0, False)
    fill_q(x_ref, head, rows, width, q_scr, 0)
    fill_back(x_ref, head, rows, width, d_scr, back_scr)
    mine = slice(head * rows, (head + 1) * rows)
    for b in range(GROUP):
        k_scr[b] = x_ref[b, mine, :].T[:width]
    own = pl.ds(head * GROUP, GROUP)
    acc[...] = jnp.zeros_like(acc)
    dq_scr[...] = dq_in[head * GROUP : (head + 1) * GROUP]
    keys = lambda b: x_ref[b, mine, :]
    back_units(total, patch_of, block_of, keys, q_scr, d_scr, back_scr, k_scr, (s0, s1), stat_ref.at[own], dq_scr, acc)
    for p in range(GROUP):
        out_ref[p, :rows, :] = acc[p].astype(BF16)
        out_ref[p, rows:, :] = beside(dq_scr[p].astype(BF16))


def merge_kernel(alone, *refs):
    owns, back_ref, attn_ref, out_ref = refs[:MINE], refs[MINE], refs[-2], refs[-1]
    each = owns[0].shape[1]
    rows = each * 2 // 3
    for p in range(GROUP):
        out_ref[p, MINE * each :, :] = attn_ref[p]
    for i in range(MINE):
        for p in range(GROUP):
            out_ref[p, i * each : (i + 1) * each, :] = owns[i][p]
        mine = slice(i * each, i * each + rows)
        other = 1 - lax.axis_index("seg") // GROUP if alone else 0
        for side in range(back_ref.shape[0] // REACH):
            start = other if alone else 1 - side
            for j in range(REACH):
                term = back_ref[side * REACH + j, i * rows : (i + 1) * rows, :].astype(F32)
                here = out_ref[start + j, mine, :].astype(F32)
                out_ref[start + j, mine, :] = (here + term).astype(BF16)


def unpack_kernel(y_ref, w_ref, out_ref, dq_ref, dk_ref, dv_ref):
    rows, width = dk_ref.shape[0], y_ref.shape[2] // 2
    half = rows // 2
    sides = ([], [])
    for h in range(HEADS):
        cols = slice(h * width, (h + 1) * width)
        r, i = divmod(h, MINE)
        at = i * (rows + half)
        dk_ref[:, cols] = y_ref[r, at : at + rows, :width]
        dv_ref[:, cols] = y_ref[r, at : at + rows, width:]
        dq_ref[:half, cols] = y_ref[r, at + rows : at + rows + half, :width]
        dq_ref[half:, cols] = y_ref[r, at + rows : at + rows + half, width:]
        at = MINE * (rows + half) + i * half
        sides[0].append(y_ref[r, at : at + half, :width])
        sides[1].append(y_ref[r, at : at + half, width:])
    attn = jnp.concatenate([jnp.concatenate(side, axis=1) for side in sides], axis=0)
    out_ref[...] = mm(attn, w_ref[...]).astype(BF16)


def params(mib=32):
    return pltpu.CompilerParams(vmem_limit_bytes=mib * 2**20)


def cost(flops, bytes_accessed, exps=0):
    return pl.CostEstimate(flops=flops // 1000, bytes_accessed=bytes_accessed // 1000, transcendentals=0)


def in_hbm(array):
    return pltpu.with_memory_space_constraint(array, pltpu.HBM)


def around(count, by):
    return [(i, (i + by) % count) for i in range(count)]


def exchange(pieces, axis):
    count = pieces.shape[0]
    if count > HEADS:
        return lax.all_to_all(pieces, axis, 0, 0)
    here = lax.axis_index(axis)
    arrived = []
    for by in range(count):
        piece = lax.dynamic_index_in_dim(pieces, (here + by) % count, 0, keepdims=False)
        arrived.append(lax.ppermute(piece, axis, around(count, by)) if by else piece)
    return jnp.stack(arrived)


def gathered(piece, axis, count):
    size = lax.axis_size(axis)
    here = lax.axis_index(axis) % count
    arrived = [piece]
    for by in range(1, count):
        pairs = [(i, i // count * count + (i + by) % count) for i in range(size)]
        arrived.append(lax.ppermute(piece, axis, pairs))
    line = jnp.stack(arrived[::-1] + arrived[::-1])
    return lax.dynamic_slice_in_dim(line, count - 1 - here, count, 0)


def body(queries, key_rows, value_rows, w_out, grad_out, neighbours):
    _, rows, model = queries.shape
    width = model // HEADS
    half, wide = rows // 2, 2 * width
    seg = lax.axis_size("seg")
    samples = lax.axis_size("sample")
    groups = seg // GROUP
    split = [[g * GROUP + i for i in range(GROUP)] for g in range(groups)]
    alone = groups == 2
    halo = REACH if alone else 2 * REACH
    ones = 16
    most = GROUP * (NBR + 1)
    vmem = pl.BlockSpec(memory_space=pltpu.VMEM)
    smem = pl.BlockSpec(memory_space=pltpu.SMEM)
    unit_cost = rows * rows

    def swap(array):
        return lax.all_to_all(array, "seg", 0, 0, axis_index_groups=split)

    def shifted(array, by):
        pairs = [(s, s + by) for s in range(seg) if 0 <= s + by < seg]
        return lax.ppermute(array, "seg", pairs)

    def across(array):
        return lax.ppermute(array, "seg", [(s, (s + GROUP) % seg) for s in range(seg)])

    def between(array):
        pairs = [[i, i + GROUP] for i in range(GROUP)]
        return lax.all_to_all(array, "seg", 0, 0, axis_index_groups=pairs)

    def call(kernel, name, outs, scratch, flops, exps=0, mib=32):
        return pl.pallas_call(
            kernel,
            out_shape=[jax.ShapeDtypeStruct(shape, kind) for shape, kind in outs],
            out_specs=[vmem] * len(outs),
            scratch_shapes=scratch,
            compiler_params=params(mib),
            cost_estimate=cost(flops, 4 * 2**20, exps),
            name=name,
        )

    packed, *direct = pl.pallas_call(
        pack_kernel,
        in_specs=[smem] + [pl.BlockSpec(memory_space=pltpu.HBM)] * 5,
        scratch_shapes=[pltpu.VMEM((rows, model), BF16)] * 4
        + [pltpu.VMEM((model, model), BF16), pltpu.SemaphoreType.DMA((5,))],
        out_shape=[
            jax.ShapeDtypeStruct((GROUP, MINE * (rows + 2 * half) + 16, wide), BF16),
        ]
        + [jax.ShapeDtypeStruct((MINE * rows, wide), BF16)] * (GROUP if alone else 0),
        compiler_params=params(60),
        cost_estimate=cost(2 * rows * model * model, 10 * rows * model),
        name="pack",
    )(
        neighbours[0],
        *(in_hbm(a) for a in (queries[0], key_rows[0], value_rows[0], grad_out[0], w_out)),
    )
    x = swap(packed)
    if alone:
        border = [g * GROUP + i for g in range(2) for i in range(1 - g, 1 - g + REACH)]
        beyond = [
            lax.ppermute(array, "seg", [(s, (s + GROUP) % seg ^ by) for s in border])
            for by, array in enumerate(direct)
        ]
    else:
        kv = x[:, : MINE * rows]
        beyond = [
            jnp.concatenate([shifted(kv[1:], GROUP), shifted(kv[:REACH], -GROUP)], axis=0)
        ]
    at = MINE * (rows + 2 * half)
    near = x[:, at : at + NBR, 0].astype(jnp.int32)
    x, near, beyond, grad_in = lax.optimization_barrier((x, near, beyond, grad_out[0]))
    grads_here = [grad_in] + [
        lax.ppermute(grad_in, "seg", [(s, s ^ by) for s in range(seg)]) for by in range(1, GROUP)
    ]

    lists = lambda count: [pltpu.SMEM((count + 8,), jnp.int32)] * 2
    sheet = pltpu.VMEM((rows, rows), F32)
    double = pltpu.VMEM((rows, 2 * rows), F32)
    lines = lambda count: pltpu.VMEM((count, 1, rows), F32)
    patches = MINE * GROUP
    blocks = GROUP + halo
    attn, stat, dq, far = call(
        functools.partial(attend_kernel, alone),
        "attend",
        [
            ((GROUP, MINE * half, wide), BF16),
            ((patches, 2, rows), F32),
            ((patches, width, rows), F32),
            ((halo, MINE * rows, wide), BF16),
        ],
        [
            pltpu.VMEM((MINE * blocks, rows, wide), F32),
            double,
            double,
            lines(MINE * most),
            lines(MINE * most),
            lines(patches),
            pltpu.VMEM((patches, width + ones, rows), F32),
            pltpu.VMEM((patches, wide, rows), BF16),
            pltpu.VMEM((patches, wide, rows), BF16),
            pltpu.VMEM((patches, 2 * rows, wide), BF16),
            pltpu.VMEM((MINE * blocks, width + ones, rows), BF16),
            pltpu.VMEM((MINE * blocks, width, rows), BF16),
            pltpu.VMEM((blocks, MINE * rows, wide), BF16),
        ]
        + lists(MINE * most)
        + lists(MINE * most),
        6 * unit_cost * 1536,
        12 * unit_cost,
        60,
    )(near, x, *beyond)
    if alone:
        back = across(far)
    else:
        back = jnp.concatenate([shifted(far[:REACH], -GROUP), shifted(far[REACH:], GROUP)], axis=0)

    def own_terms(i, stat, dq):
        return call(
            functools.partial(own_kernel, i),
            f"own{i}",
            [((GROUP, rows + half, wide), BF16)],
            [
                pltpu.VMEM((GROUP, rows, wide), F32),
                double,
                double,
                pltpu.VMEM((GROUP, width, rows), F32),
                pltpu.VMEM((GROUP, wide, rows), BF16),
                pltpu.VMEM((GROUP, wide, rows), BF16),
                pltpu.VMEM((GROUP, 2 * rows, wide), BF16),
                pltpu.VMEM((GROUP, width, rows), BF16),
            ]
            + lists(most),
            10 * unit_cost * 1280,
            10 * unit_cost,
        )(near, x, stat, dq)[0]

    part = MINE * width // samples
    (w_term,) = call(
        term_kernel, "term", [((MINE * width, model), BF16)], [], 2 * rows * model * model
    )(attn, *grads_here)
    w_part = exchange(w_term.reshape(samples, part, model), "sample")
    w_part = jnp.sum(w_part.astype(F32), axis=0).astype(BF16)
    own0 = own_terms(0, stat, dq)
    w_part, stat, own0 = lax.optimization_barrier((w_part, stat, own0))
    own1 = own_terms(1, stat, dq)
    if alone:
        w_part = w_part.astype(F32) + across(w_part).astype(F32)
    else:
        alike = [[g * GROUP + r for g in range(groups)] for r in range(GROUP)]
        w_part = lax.psum(w_part.astype(F32), "seg", axis_index_groups=alike)
    w_part, back, own1 = lax.optimization_barrier((w_part, back, own1))
    (merged,) = call(
        functools.partial(merge_kernel, alone),
        "merge",
        [((GROUP, MINE * (rows + 2 * half), wide), BF16)],
        [],
        0,
    )(own0, own1, back, attn)
    w_part, merged = lax.optimization_barrier((w_part, merged))
    home = swap(merged)
    grad_scale = 1.0 / math.sqrt(samples * rows * seg)
    w_rows = gathered((w_part * grad_scale).astype(BF16), "seg", GROUP)
    w_all = gathered(w_rows, "sample", samples)
    grad_w_out = jnp.transpose(w_all, (1, 0, 2, 3)).reshape(model, model).astype(F32)
    attended, grad_q, grad_k, grad_v = call(
        unpack_kernel, "unpack", [((rows, model), BF16)] * 4, [], 2 * rows * model * model
    )(home, w_out)
    return attended[None], grad_q[None], grad_k[None], grad_v[None], grad_w_out


def solution(mesh):
    rows = P("sample", "seg", None)
    return jax.shard_map(
        body,
        mesh=mesh,
        in_specs=(rows, rows, rows, P(), rows, rows),
        out_specs=(rows, rows, rows, rows, P()),
        check_vma=False,
    )
```

```python
import functools
import math

import jax
import jax.numpy as jnp
from jax import lax
from jax.experimental import pallas as pl
from jax.experimental.pallas import tpu as pltpu
from jax.sharding import PartitionSpec as P

HEADS = 8
NBR = 3
REACH = 3
GROUP = 4
MINE = HEADS // GROUP
F32 = jnp.float32
BF16 = jnp.bfloat16


def mm(a, b):
    return lax.dot_general(a, b, (((1,), (0,)), ((), ())), preferred_element_type=F32)


def halves(block):
    turned = block.T
    width = turned.shape[0] // 2
    return jnp.concatenate([turned[:width], turned[width:]], axis=1)


def beside(turned):
    rows = turned.shape[1]
    return jnp.concatenate([turned[:, : rows // 2], turned[:, rows // 2 :]], axis=0).T


def pack_kernel(near_ref, *refs):
    sources, (out_ref, *direct), held, arrived = refs[:5], refs[5:-6], refs[-6:-1], refs[-1]
    copies = [
        pltpu.make_async_copy(source, target, arrived.at[i])
        for i, (source, target) in enumerate(zip(sources, held))
    ]
    for copy in copies:
        copy.start()
    for copy in copies:
        copy.wait()
    q_ref, k_ref, v_ref, g_ref, w_ref = held
    rows = q_ref.shape[0]
    width = q_ref.shape[1] // HEADS
    half = rows // 2
    here = lax.axis_index("seg")
    line = lax.broadcasted_iota(jnp.int32, (16, 2 * width), 0)
    offsets = jnp.zeros((16, 2 * width), F32)
    for e in range(NBR):
        offsets = jnp.where(line == e, (near_ref[0, e] - here + REACH).astype(F32), offsets)
    d_attn = lax.dot_general(
        g_ref[...], w_ref[...], (((1,), (1,)), ((), ())), preferred_element_type=F32
    ).astype(BF16)
    for h in range(HEADS):
        to, i = divmod(h, MINE)
        cols = slice(h * width, (h + 1) * width)
        at_q = MINE * rows + i * half
        at_d = MINE * (rows + half) + i * half
        out_ref[to, i * rows : (i + 1) * rows, :] = jnp.concatenate(
            [k_ref[:, cols], v_ref[:, cols]], axis=1
        )
        out_ref[to, at_q : at_q + half, :] = jnp.concatenate(
            [q_ref[:half, cols], q_ref[half:, cols]], axis=1
        )
        out_ref[to, at_d : at_d + half, :] = jnp.concatenate(
            [d_attn[:half, cols], d_attn[half:, cols]], axis=1
        )
        out_ref[to, MINE * (rows + 2 * half) :, :] = offsets.astype(BF16)
    for by, ref in enumerate(direct):
        ref[...] = out_ref[(here % GROUP) ^ by, : MINE * rows, :]


def list_units(near_ref, patch_of, block_of, count, first, outside, right=0, base=0):
    for p in range(GROUP):
        if not outside:
            patch_of[count] = first + p
            block_of[count] = base + p
            count = count + 1
        for e in range(NBR):
            t = p + near_ref[p, e] - REACH
            inside = jnp.logical_and(t >= 0, t < GROUP)
            patch_of[count] = first + p
            if outside:
                want = jnp.logical_not(inside)
                block_of[count] = base + jnp.where(t < 0, t + REACH, t - GROUP + right)
            else:
                want = jnp.logical_and(inside, t != p)
                block_of[count] = base + t
            count = count + jnp.where(want, 1, 0)
    return count


def in_turn(total, enter, leave):
    def both(u, slot):
        leave(u, slot, lambda: enter(u + 1, 1 - slot))

    def two(i, carry):
        both(2 * i, 0)
        both(2 * i + 1, 1)
        return carry

    @pl.when(total > 0)
    def _():
        enter(jnp.int32(0), 0)
        lax.fori_loop(0, (total - 1) // 2, two, 0)
        pl.when(total % 2 == 0)(lambda: both(total - 2, 0))
        for slot in range(2):

            @pl.when((total - 1) % 2 == slot)
            def _():
                leave(total - 1, slot, lambda: None)


def mix_units(total, patch_of, block_of, keys, q_scr, v_scr, scores, before_scr, top_scr, m_ref, o_ref):
    def enter(u, slot):
        p = patch_of[u]
        s = mm(keys(block_of[u]), q_scr[p])
        scores[slot][...] = s
        before = m_ref[p]
        top = jnp.maximum(before, jnp.max(s, axis=0, keepdims=True))
        before_scr[u] = before
        top_scr[u] = top
        m_ref[p] = top

    def leave(u, slot, then):
        p, top = patch_of[u], top_scr[u]
        prob = jnp.exp(scores[slot][...] - top).astype(BF16)
        keep = jnp.exp(before_scr[u] - top)
        then()
        o_ref[p] = o_ref[p] * keep + mm(v_scr[block_of[u]], prob)

    in_turn(total, enter, leave)


def back_units(total, patch_of, block_of, keys, q_scr, d_scr, back_scr, k_scr, pairs, stat_ref, dq_ref, acc):
    rows = q_scr.shape[2]

    def enter(u, slot):
        block, p = keys(block_of[u]), patch_of[u]
        pairs[slot][:, :rows] = mm(block, q_scr[p])
        pairs[slot][:, rows:] = mm(block, d_scr[p])

    def leave(u, slot, then):
        b, p = block_of[u], patch_of[u]
        prob = jnp.exp(pairs[slot][:, :rows] - stat_ref[p, :1])
        ds = (prob * (pairs[slot][:, rows:] - stat_ref[p, 1:])).astype(BF16)
        then()
        dq_ref[p] += mm(k_scr[b], ds)
        acc[b] += mm(jnp.concatenate([ds, prob.astype(BF16)], axis=1), back_scr[p])

    in_turn(total, enter, leave)


def fill_q(x_ref, head, rows, width, q_scr, at):
    half = rows // 2
    start = MINE * rows + head * half
    for p in range(GROUP):
        turned = halves(x_ref[p, start : start + half, :])
        q_scr[at + p, :width, :] = turned * BF16(1.0 / math.sqrt(width))
        q_scr[at + p, width:, :] = jnp.zeros_like(turned)


def fill_back(x_ref, head, rows, width, d_scr, back_scr, at=0):
    half = rows // 2
    start = MINE * rows + head * half
    blank = jnp.zeros((half, width), BF16)
    for p in range(GROUP):
        q_pair = x_ref[p, start : start + half, :]
        d_pair = x_ref[p, start + MINE * half : start + (MINE + 1) * half, :]
        back_scr[at + p, :half, :] = jnp.concatenate([q_pair[:, :width], blank], axis=1)
        back_scr[at + p, half:rows, :] = jnp.concatenate([q_pair[:, width:], blank], axis=1)
        back_scr[at + p, rows : rows + half, :] = jnp.concatenate([blank, d_pair[:, :width]], axis=1)
        back_scr[at + p, rows + half :, :] = jnp.concatenate([blank, d_pair[:, width:]], axis=1)
        d_turned = halves(d_pair)
        d_scr[at + p, :width, :] = jnp.zeros_like(d_turned)
        d_scr[at + p, width:, :] = d_turned * BF16(1.0 / math.sqrt(width))


def attend_kernel(alone, near_ref, x_ref, *refs):
    halos, refs = refs[: GROUP if alone else 1], refs[GROUP if alone else 1 :]
    (attn_ref, stat_ref, dq_ref, out_ref, acc, s0, s1, before_scr, top_scr, m_scr, o_scr, q_scr, d_scr, back_scr, v_scr, k_scr, kv_scr, patch_of, block_of, far_patch, far_block) = refs
    rows, width = q_scr.shape[2], x_ref.shape[2] // 2
    half, halo = rows // 2, REACH if alone else 2 * REACH
    blocks = GROUP + halo
    right = halo - REACH
    other = 1 - lax.axis_index("seg") // GROUP if alone else 0
    for b in range(GROUP):
        kv_scr[b] = x_ref[b, : MINE * rows, :]
    for b in range(halo):
        if alone:
            by = (b + 1 - other) ^ (lax.axis_index("seg") % GROUP)
            for k in range(GROUP):

                @pl.when(by == k)
                def _():
                    kv_scr[GROUP + b] = halos[k][...]

        else:
            kv_scr[GROUP + b] = halos[0][b]
    total, far_total = jnp.int32(0), jnp.int32(0)
    for i in range(MINE):
        base = i * blocks
        total = list_units(near_ref, patch_of, block_of, total, i * GROUP, False, 0, base)
        total = list_units(near_ref, patch_of, block_of, total, i * GROUP, True, right, base + GROUP)
        far_total = list_units(
            near_ref, far_patch, far_block, far_total, i * GROUP, True, right, base + GROUP
        )
        fill_q(x_ref, i, rows, width, q_scr, i * GROUP)
        fill_back(x_ref, i, rows, width, d_scr, back_scr, i * GROUP)
        for b in range(blocks):
            turned = kv_scr[b, i * rows : (i + 1) * rows, :].T
            v_scr[base + b, :width, :] = turned[width:]
            v_scr[base + b, width:, :] = jnp.ones((v_scr.shape[1] - width, rows), BF16)
            if b >= GROUP:
                k_scr[base + b] = turned[:width]
    o_scr[...] = jnp.zeros_like(o_scr)
    m_scr[...] = jnp.full_like(m_scr, -jnp.inf)

    def keys(b):
        return kv_scr[b % blocks, pl.ds(pl.multiple_of(b // blocks * rows, rows), rows), :]

    firsts = (s0.at[:, :rows], s1.at[:, :rows])
    mix_units(total, patch_of, block_of, keys, q_scr, v_scr, firsts, before_scr, top_scr, m_scr, o_scr)
    for p in range(MINE * GROUP):
        sums = o_scr[p, width : width + 1, :]
        attn = (o_scr[p, :width, :] * (1.0 / sums)).astype(BF16)
        attn_ref[p % GROUP, p // GROUP * half : (p // GROUP + 1) * half, :] = beside(attn)
        stat_ref[p, :1] = m_scr[p] + jnp.log(sums)
        product = d_scr[p, width:, :].astype(F32) * attn.astype(F32)
        stat_ref[p, 1:] = jnp.sum(product, axis=0, keepdims=True)
    for i in range(MINE):
        for b in range(halo):
            acc[i * blocks + GROUP + b] = jnp.zeros(acc.shape[1:], F32)
    dq_ref[...] = jnp.zeros_like(dq_ref)
    back_units(far_total, far_patch, far_block, keys, q_scr, d_scr, back_scr, k_scr, (s0, s1), stat_ref, dq_ref, acc)
    for i in range(MINE):
        for b in range(halo):
            out_ref[b, i * rows : (i + 1) * rows, :] = acc[i * blocks + GROUP + b].astype(BF16)


def term_kernel(attn_ref, *refs):
    grads, term_ref = refs[:GROUP], refs[GROUP]
    half = attn_ref.shape[1] // MINE
    term = jnp.zeros(term_ref.shape, F32)
    for by in range(GROUP):
        p = (lax.axis_index("seg") % GROUP) ^ by
        turned = [halves(attn_ref[p, i * half : (i + 1) * half, :]) for i in range(MINE)]
        term = term + mm(jnp.concatenate(turned, axis=0), grads[by][...])
    term_ref[...] = term.astype(BF16)


def own_kernel(head, near_ref, x_ref, stat_ref, dq_in, out_ref, acc, s0, s1, dq_scr, q_scr, d_scr, back_scr, k_scr, patch_of, block_of):
    rows, width = q_scr.shape[2], x_ref.shape[2] // 2
    total = list_units(near_ref, patch_of, block_of, jnp.int32(0), 0, False)
    fill_q(x_ref, head, rows, width, q_scr, 0)
    fill_back(x_ref, head, rows, width, d_scr, back_scr)
    mine = slice(head * rows, (head + 1) * rows)
    for b in range(GROUP):
        k_scr[b] = x_ref[b, mine, :].T[:width]
    own = pl.ds(head * GROUP, GROUP)
    acc[...] = jnp.zeros_like(acc)
    dq_scr[...] = dq_in[head * GROUP : (head + 1) * GROUP]
    keys = lambda b: x_ref[b, mine, :]
    back_units(total, patch_of, block_of, keys, q_scr, d_scr, back_scr, k_scr, (s0, s1), stat_ref.at[own], dq_scr, acc)
    for p in range(GROUP):
        out_ref[p, :rows, :] = acc[p].astype(BF16)
        out_ref[p, rows:, :] = beside(dq_scr[p].astype(BF16))


def merge_kernel(alone, *refs):
    owns, back_ref, attn_ref, out_ref = refs[:MINE], refs[MINE], refs[-2], refs[-1]
    each = owns[0].shape[1]
    rows = each * 2 // 3
    for p in range(GROUP):
        out_ref[p, MINE * each :, :] = attn_ref[p]
    for i in range(MINE):
        for p in range(GROUP):
            out_ref[p, i * each : (i + 1) * each, :] = owns[i][p]
        mine = slice(i * each, i * each + rows)
        other = 1 - lax.axis_index("seg") // GROUP if alone else 0
        for side in range(back_ref.shape[0] // REACH):
            start = other if alone else 1 - side
            for j in range(REACH):
                term = back_ref[side * REACH + j, i * rows : (i + 1) * rows, :].astype(F32)
                here = out_ref[start + j, mine, :].astype(F32)
                out_ref[start + j, mine, :] = (here + term).astype(BF16)


def unpack_kernel(y_ref, w_ref, out_ref, dq_ref, dk_ref, dv_ref):
    rows, width = dk_ref.shape[0], y_ref.shape[2] // 2
    half = rows // 2
    sides = ([], [])
    for h in range(HEADS):
        cols = slice(h * width, (h + 1) * width)
        r, i = divmod(h, MINE)
        at = i * (rows + half)
        dk_ref[:, cols] = y_ref[r, at : at + rows, :width]
        dv_ref[:, cols] = y_ref[r, at : at + rows, width:]
        dq_ref[:half, cols] = y_ref[r, at + rows : at + rows + half, :width]
        dq_ref[half:, cols] = y_ref[r, at + rows : at + rows + half, width:]
        at = MINE * (rows + half) + i * half
        sides[0].append(y_ref[r, at : at + half, :width])
        sides[1].append(y_ref[r, at : at + half, width:])
    attn = jnp.concatenate([jnp.concatenate(side, axis=1) for side in sides], axis=0)
    out_ref[...] = mm(attn, w_ref[...]).astype(BF16)


def params(mib=32):
    return pltpu.CompilerParams(vmem_limit_bytes=mib * 2**20)


def cost(flops, bytes_accessed, exps=0):
    return pl.CostEstimate(flops=flops // 1000, bytes_accessed=bytes_accessed // 1000, transcendentals=0)


def in_hbm(array):
    return pltpu.with_memory_space_constraint(array, pltpu.HBM)


def around(count, by):
    return [(i, (i + by) % count) for i in range(count)]


def exchange(pieces, axis):
    count = pieces.shape[0]
    if count > HEADS:
        return lax.all_to_all(pieces, axis, 0, 0)
    here = lax.axis_index(axis)
    arrived = []
    for by in range(count):
        piece = lax.dynamic_index_in_dim(pieces, (here + by) % count, 0, keepdims=False)
        arrived.append(lax.ppermute(piece, axis, around(count, by)) if by else piece)
    return jnp.stack(arrived)


def gathered(piece, axis, count):
    size = lax.axis_size(axis)
    here = lax.axis_index(axis) % count
    arrived = [piece]
    for by in range(1, count):
        pairs = [(i, i // count * count + (i + by) % count) for i in range(size)]
        arrived.append(lax.ppermute(piece, axis, pairs))
    line = jnp.stack(arrived[::-1] + arrived[::-1])
    return lax.dynamic_slice_in_dim(line, count - 1 - here, count, 0)


def body(queries, key_rows, value_rows, w_out, grad_out, neighbours):
    _, rows, model = queries.shape
    width = model // HEADS
    half, wide = rows // 2, 2 * width
    seg = lax.axis_size("seg")
    samples = lax.axis_size("sample")
    groups = seg // GROUP
    split = [[g * GROUP + i for i in range(GROUP)] for g in range(groups)]
    alone = groups == 2
    halo = REACH if alone else 2 * REACH
    ones = 16
    most = GROUP * (NBR + 1)
    vmem = pl.BlockSpec(memory_space=pltpu.VMEM)
    smem = pl.BlockSpec(memory_space=pltpu.SMEM)
    unit_cost = rows * rows

    def swap(array):
        return lax.all_to_all(array, "seg", 0, 0, axis_index_groups=split)

    def shifted(array, by):
        pairs = [(s, s + by) for s in range(seg) if 0 <= s + by < seg]
        return lax.ppermute(array, "seg", pairs)

    def across(array):
        return lax.ppermute(array, "seg", [(s, (s + GROUP) % seg) for s in range(seg)])

    def between(array):
        pairs = [[i, i + GROUP] for i in range(GROUP)]
        return lax.all_to_all(array, "seg", 0, 0, axis_index_groups=pairs)

    def call(kernel, name, outs, scratch, flops, exps=0, mib=32):
        return pl.pallas_call(
            kernel,
            out_shape=[jax.ShapeDtypeStruct(shape, kind) for shape, kind in outs],
            out_specs=[vmem] * len(outs),
            scratch_shapes=scratch,
            compiler_params=params(mib),
            cost_estimate=cost(flops, 4 * 2**20, exps),
            name=name,
        )

    packed, *direct = pl.pallas_call(
        pack_kernel,
        in_specs=[smem] + [pl.BlockSpec(memory_space=pltpu.HBM)] * 5,
        scratch_shapes=[pltpu.VMEM((rows, model), BF16)] * 4
        + [pltpu.VMEM((model, model), BF16), pltpu.SemaphoreType.DMA((5,))],
        out_shape=[
            jax.ShapeDtypeStruct((GROUP, MINE * (rows + 2 * half) + 16, wide), BF16),
        ]
        + [jax.ShapeDtypeStruct((MINE * rows, wide), BF16)] * (GROUP if alone else 0),
        compiler_params=params(60),
        cost_estimate=cost(2 * rows * model * model, 10 * rows * model),
        name="pack",
    )(
        neighbours[0],
        *(in_hbm(a) for a in (queries[0], key_rows[0], value_rows[0], grad_out[0], w_out)),
    )
    x = swap(packed)
    if alone:
        border = [g * GROUP + i for g in range(2) for i in range(1 - g, 1 - g + REACH)]
        beyond = [
            lax.ppermute(direct[by], "seg", [(s, (s + GROUP) % seg ^ by) for s in border])
            for by in reversed(range(GROUP))
        ][::-1]
    else:
        kv = x[:, : MINE * rows]
        beyond = [
            jnp.concatenate([shifted(kv[1:], GROUP), shifted(kv[:REACH], -GROUP)], axis=0)
        ]
    at = MINE * (rows + 2 * half)
    near = x[:, at : at + NBR, 0].astype(jnp.int32)
    x, near, beyond, grad_in = lax.optimization_barrier((x, near, beyond, grad_out[0]))
    grads_here = [grad_in] + [
        lax.ppermute(grad_in, "seg", [(s, s ^ by) for s in range(seg)]) for by in range(1, GROUP)
    ]

    lists = lambda count: [pltpu.SMEM((count + 8,), jnp.int32)] * 2
    sheet = pltpu.VMEM((rows, rows), F32)
    double = pltpu.VMEM((rows, 2 * rows), F32)
    lines = lambda count: pltpu.VMEM((count, 1, rows), F32)
    patches = MINE * GROUP
    blocks = GROUP + halo
    attn, stat, dq, far = call(
        functools.partial(attend_kernel, alone),
        "attend",
        [
            ((GROUP, MINE * half, wide), BF16),
            ((patches, 2, rows), F32),
            ((patches, width, rows), F32),
            ((halo, MINE * rows, wide), BF16),
        ],
        [
            pltpu.VMEM((MINE * blocks, rows, wide), F32),
            double,
            double,
            lines(MINE * most),
            lines(MINE * most),
            lines(patches),
            pltpu.VMEM((patches, width + ones, rows), F32),
            pltpu.VMEM((patches, wide, rows), BF16),
            pltpu.VMEM((patches, wide, rows), BF16),
            pltpu.VMEM((patches, 2 * rows, wide), BF16),
            pltpu.VMEM((MINE * blocks, width + ones, rows), BF16),
            pltpu.VMEM((MINE * blocks, width, rows), BF16),
            pltpu.VMEM((blocks, MINE * rows, wide), BF16),
        ]
        + lists(MINE * most)
        + lists(MINE * most),
        6 * unit_cost * 1536,
        12 * unit_cost,
        60,
    )(near, x, *beyond)
    if alone:
        back = across(far)
    else:
        back = jnp.concatenate([shifted(far[:REACH], -GROUP), shifted(far[REACH:], GROUP)], axis=0)

    def own_terms(i, stat, dq):
        return call(
            functools.partial(own_kernel, i),
            f"own{i}",
            [((GROUP, rows + half, wide), BF16)],
            [
                pltpu.VMEM((GROUP, rows, wide), F32),
                double,
                double,
                pltpu.VMEM((GROUP, width, rows), F32),
                pltpu.VMEM((GROUP, wide, rows), BF16),
                pltpu.VMEM((GROUP, wide, rows), BF16),
                pltpu.VMEM((GROUP, 2 * rows, wide), BF16),
                pltpu.VMEM((GROUP, width, rows), BF16),
            ]
            + lists(most),
            10 * unit_cost * 1280,
            10 * unit_cost,
        )(near, x, stat, dq)[0]

    part = MINE * width // samples
    (w_term,) = call(
        term_kernel, "term", [((MINE * width, model), BF16)], [], 2 * rows * model * model
    )(attn, *grads_here)
    w_part = exchange(w_term.reshape(samples, part, model), "sample")
    w_part = jnp.sum(w_part.astype(F32), axis=0).astype(BF16)
    own0 = own_terms(0, stat, dq)
    w_part, stat, own0 = lax.optimization_barrier((w_part, stat, own0))
    own1 = own_terms(1, stat, dq)
    if alone:
        w_part = w_part.astype(F32) + across(w_part).astype(F32)
    else:
        alike = [[g * GROUP + r for g in range(groups)] for r in range(GROUP)]
        w_part = lax.psum(w_part.astype(F32), "seg", axis_index_groups=alike)
    w_part, back, own1 = lax.optimization_barrier((w_part, back, own1))
    (merged,) = call(
        functools.partial(merge_kernel, alone),
        "merge",
        [((GROUP, MINE * (rows + 2 * half), wide), BF16)],
        [],
        0,
    )(own0, own1, back, attn)
    w_part, merged = lax.optimization_barrier((w_part, merged))
    home = swap(merged)
    grad_scale = 1.0 / math.sqrt(samples * rows * seg)
    w_rows = gathered((w_part * grad_scale).astype(BF16), "seg", GROUP)
    w_all = gathered(w_rows, "sample", samples)
    grad_w_out = jnp.transpose(w_all, (1, 0, 2, 3)).reshape(model, model).astype(F32)
    attended, grad_q, grad_k, grad_v = call(
        unpack_kernel, "unpack", [((rows, model), BF16)] * 4, [], 2 * rows * model * model
    )(home, w_out)
    return attended[None], grad_q[None], grad_k[None], grad_v[None], grad_w_out


def solution(mesh):
    rows = P("sample", "seg", None)
    return jax.shard_map(
        body,
        mesh=mesh,
        in_specs=(rows, rows, rows, P(), rows, rows),
        out_specs=(rows, rows, rows, rows, P()),
        check_vma=False,
    )
```
